128 devices in a mesh: gx: 16 (over x, y), gy: 8 (over z, core).
Axes of the slice: x: 4, y: 4, z: 4, core: 2. Of those that a mesh axis runs over, the one named last changes fastest.
Arguments:
- fractions: float32 [16, 8, 3, 1024], P('gx', 'gy'), may hold values from 0 to 1
- velocity: float32 [16, 8, 3, 1024], P('gx', 'gy'), may hold values from -4 to 4
- drag_rate: float32 [16, 8, 1024], P('gx', 'gy'), may hold values from 0.5 to 4
- volume: float32 [16, 8, 1024], P('gx', 'gy'), may hold values from 0.25 to 1
- owner: int32 [16, 8, 1024, 1], P('gx', 'gy'), may hold values from 0 to 127, as said below
- element: int32 [16, 8, 1024], P('gx', 'gy'), may hold values from 0 to 31
- coords: int32 [16, 8, 3, 1024], P('gx', 'gy'), may hold values from 0 to 63
- fluid: bfloat16 [16, 8, 32, 6, 512], P('gx', 'gy'), may hold values from -4 to 4
Outputs:
- particle_force: float32 [16, 8, 3, 1024], P('gx', 'gy')
- bin_field: float32 [4, 256, 128, 512], P(None, 'gx', 'gy')
The draws below stay inside these ranges and needn't reach their ends.
Inputs may be any that keep to these rules, and one draw needn't show every extreme that they name: owner names a device as its gx index times the number of gy indices plus its gy index: the particle's own device or one whose gx and gy indices each differ from it by at most one (no wrap). A particle owned by a device with gx index one lower has first fraction below 0.2, one higher at least 0.8, the same gx index from 0.2 to 0.8; likewise for gy and the second fraction. Among one device's 1024 particles at most 64 have any one other device as owner, and in every device exactly 64 have one of them.
All inputs are finite; a program needn't handle non-finite values.
Results may differ from the reference program's by a relative error of at most 0.00099.
Values may be sent and summed in bfloat16 or wider, within the bound.
A program may use at most 64 MiB of HBM per device.

```python
import math
import jax
import jax.numpy as jnp
import numpy as np
from jax import lax

P_DEV = 1024
E_DEV = 32
BINS_THIRD_AXIS = 512
BX = 16
BY = 16
MARGIN = 4
QUANT = 64
CAP = 64
N_GX = 16
N_GY = 8


def neighbour_codes(key):
    base = jax.random.fold_in(key, 7301)
    count_key, order_key = jax.random.split(base)
    grid_i = jnp.arange(N_GX, dtype=jnp.int32)[:, None, None]
    grid_j = jnp.arange(N_GY, dtype=jnp.int32)[None, :, None]
    offsets = jnp.arange(9, dtype=jnp.int32)[None, None, :]
    step_x = offsets // 3 - 1
    step_y = offsets % 3 - 1
    valid = (grid_i + step_x >= 0) & (grid_i + step_x < N_GX) & (grid_j + step_y >= 0) & (grid_j + step_y < N_GY) & (offsets != 4)
    counts = jax.random.randint(count_key, (N_GX, N_GY, 9), 1, CAP + 1).astype(jnp.int32)
    leading = valid & (jnp.cumsum(valid.astype(jnp.int32), axis=2) == 1)
    counts = jnp.where(leading, CAP, counts)
    counts = jnp.where(valid, counts, 0)
    remainder = P_DEV - jnp.sum(counts, axis=2, keepdims=True)
    counts = jnp.where(offsets == 4, remainder, counts)
    bounds = jnp.cumsum(counts, axis=2)
    rows = jnp.arange(P_DEV, dtype=jnp.int32)[None, None, :, None]
    sorted_codes = jnp.sum((rows >= bounds[:, :, None, :]).astype(jnp.int32), axis=3)
    keys = jax.random.split(order_key, N_GX * N_GY)

    def shuffle(single):
        return jax.random.permutation(single, P_DEV)
    orders = jax.vmap(shuffle)(keys).reshape(N_GX, N_GY, P_DEV).astype(jnp.int32)
    return jnp.take_along_axis(sorted_codes, orders, axis=2)


def draw_owner(key, part):
    codes = neighbour_codes(key)
    grid_i = jnp.arange(N_GX, dtype=jnp.int32)[:, None, None]
    grid_j = jnp.arange(N_GY, dtype=jnp.int32)[None, :, None]
    owner = (grid_i + codes // 3 - 1) * N_GY + grid_j + codes % 3 - 1
    return owner.reshape(N_GX, N_GY, P_DEV, 1).astype(jnp.int32)


def edge_fraction(steps, uniform_part):
    return jnp.where(steps < 0, 0.2 * uniform_part, jnp.where(steps > 0, 0.8 + 0.2 * uniform_part, 0.2 + 0.6 * uniform_part))


def draw_fractions(key, part):
    codes = neighbour_codes(key)
    step_x = codes // 3 - 1
    step_y = codes % 3 - 1
    uniform_all = jax.random.uniform(jax.random.fold_in(key, 7411), (N_GX, N_GY, 3, P_DEV), jnp.float32)
    jitter_all = jax.random.uniform(jax.random.fold_in(key, 7523), (N_GX, N_GY, 3, P_DEV), jnp.float32, -1.0, 1.0)
    cluster = jax.random.bernoulli(jax.random.fold_in(key, 7639), 0.5, (N_GX, N_GY, P_DEV))
    depth_centre = jax.random.uniform(jax.random.fold_in(key, 7757), (), jnp.float32, 0.25, 0.75)
    near_centre = 0.02
    far_centre = 0.065
    spread_x = 0.015
    edge_offset = jnp.where(cluster, far_centre, near_centre) + spread_x * jitter_all[:, :, 0]
    along_first = jnp.where(step_x < 0, edge_offset, jnp.where(step_x > 0, 1.0 - edge_offset, 0.2 + 0.6 * uniform_all[:, :, 0]))
    lane_value = 0.5 + 0.4 * step_y.astype(jnp.float32) + 0.015 * jitter_all[:, :, 1]
    along_second = jnp.where(step_x != 0, lane_value, edge_fraction(step_y, uniform_all[:, :, 1]))
    depth_value = depth_centre + 0.1 * BX / BINS_THIRD_AXIS * jitter_all[:, :, 2]
    along_third = jnp.where(step_x != 0, depth_value, uniform_all[:, :, 2])
    stacked = jnp.stack([along_first, along_second, along_third], axis=2)
    return jnp.clip(stacked, 0.0, 1.0).astype(jnp.float32)


def with_ends(array, stream_key, least, high):
    spot = [jax.random.randint(jax.random.fold_in(stream_key, axis), (), 0, length) for axis, length in enumerate(array.shape)]
    longest = array.shape.index(max(array.shape))
    next_to = spot[:longest] + [(spot[longest] + 1) % array.shape[longest]] + spot[longest + 1:]
    return array.at[tuple(spot)].set(least).at[tuple(next_to)].set(high)


def steps_of(stream_key, extent, cuts, smallest, high):
    def one(axis_at, shards_of):
        steps = jax.random.uniform(jax.random.fold_in(jax.random.fold_in(stream_key, 6), axis_at), (shards_of,), jnp.float32, smallest / len(cuts), high / len(cuts))
        return jnp.repeat(jnp.exp(steps), extent[axis_at] // shards_of).reshape((-1,) + (1,) * (len(extent) - axis_at - 1))

    factor_of = one(*cuts[0])
    for cut in cuts[1:]:
        factor_of = factor_of * one(*cut)
    return factor_of


def noise(stream_key, dims, scale, limit, cuts=(), held_as=jnp.bfloat16):
    values = scale * jax.random.normal(stream_key, dims, jnp.float32)
    if cuts:
        values = values * steps_of(stream_key, dims, cuts, -0.22, 0.18)
    return jnp.clip(values, -limit, limit).astype(held_as)


def setup_inputs(seed: int = 0) -> dict:
    key_list = jax.random.split(jax.random.key(seed), 9)
    fractions = draw_fractions(jax.random.fold_in(key_list[8], 71), 0)
    velocity = noise(key_list[1], (N_GX, N_GY, 3, P_DEV), 0.25, 4.0, ((0, 16), (1, 8)), jnp.float32)
    drag_rate = jnp.clip(jnp.exp(math.log(4.0) - 2.0794415 * jax.random.uniform(key_list[2], (N_GX, N_GY, P_DEV), jnp.float32) ** steps_of(key_list[2], (N_GX, N_GY, P_DEV), ((0, 16), (1, 8)), -0.2, 0.2)), 0.5, 4.0)
    volume = jnp.clip(jnp.exp(math.log(1.0) - 1.3862944 * jax.random.uniform(key_list[3], (N_GX, N_GY, P_DEV), jnp.float32) ** steps_of(key_list[3], (N_GX, N_GY, P_DEV), ((0, 16), (1, 8)), -0.2, 0.2)), 0.25, 1.0)
    owner = draw_owner(jax.random.fold_in(key_list[8], 71), 0)
    element = with_ends(jax.random.randint(key_list[5], (N_GX, N_GY, P_DEV), 0, E_DEV), jax.random.fold_in(key_list[5], 1), 0, E_DEV - 1).astype(jnp.int32)
    coords = with_ends(jax.random.randint(key_list[6], (N_GX, N_GY, 3, P_DEV), 0, QUANT), jax.random.fold_in(key_list[6], 1), 0, QUANT - 1).astype(jnp.int32)
    fluid = noise(key_list[7], (N_GX, N_GY, E_DEV, 6, 512), 0.25, 4.0, ((0, 16), (1, 8)))
    return dict(fractions=fractions, velocity=velocity, drag_rate=drag_rate, volume=volume, owner=owner, element=element, coords=coords, fluid=fluid)


GLL_NODES = (-1.0, -0.8717401485096066, -0.5917001814331423, -0.2092992179024789,
             0.2092992179024789, 0.5917001814331423, 0.8717401485096066, 1.0)
STIFFNESS = 0.5
PAIR_WIDTH = 0.3
FILTER_BINS = 3.0


def basis_table(levels):
    points = -1.0 + (2.0 * np.arange(levels) + 1.0) / levels
    lagrange = np.ones((levels, 8))
    for node_a in range(8):
        for node_b in range(8):
            if node_b != node_a:
                lagrange[:, node_a] *= (points - GLL_NODES[node_b]) / (GLL_NODES[node_a] - GLL_NODES[node_b])
    return jnp.asarray(lagrange, dtype=jnp.float32)


def place(fractions, slab_x, slab_y):
    return jnp.stack([slab_x + fractions[0], slab_y + fractions[1], fractions[2] * (BINS_THIRD_AXIS / BX)])


def gaussian_rows(along, centres, deviation):
    distance = along[:, None] - centres[None, :]
    bumps = jnp.exp(-(distance * distance) / (2.0 * deviation * deviation))
    return bumps / jnp.sum(bumps, axis=1, keepdims=True)


def window_spread(positions, loads, slab_x, slab_y, span_x, span_y):
    first_extent = BX + 2 * MARGIN
    second_extent = BY + 2 * MARGIN
    centre_x = slab_x + (jnp.arange(first_extent, dtype=jnp.float32) - MARGIN + 0.5) / BX
    centre_y = slab_y + (jnp.arange(second_extent, dtype=jnp.float32) - MARGIN + 0.5) / BY
    centre_z = (jnp.arange(BINS_THIRD_AXIS, dtype=jnp.float32) + 0.5) / BX
    along_x = gaussian_rows(positions[0], centre_x, FILTER_BINS / BX)[:, span_x[0]:span_x[0] + span_x[1]]
    along_y = gaussian_rows(positions[1], centre_y, FILTER_BINS / BY)[:, span_y[0]:span_y[0] + span_y[1]]
    along_depth = gaussian_rows(positions[2], centre_z, FILTER_BINS / BX).astype(jnp.bfloat16)
    plane = (along_x[:, :, None] * along_y[:, None, :]).reshape(positions.shape[1], span_x[1] * span_y[1])
    scattered_loads = (loads[:, :, None] * plane[None, :, :]).astype(jnp.bfloat16)
    return scattered_loads, along_depth


def pair_forces(own, blocks, present):
    particles = own.shape[1]
    row_count = min(512, particles)
    groups = particles // row_count
    stacked = own.reshape(3, groups, row_count).transpose(1, 0, 2)

    def one_group(subset):
        summed = jnp.zeros((3, row_count), own.dtype)
        for ghost_block, weight in zip(blocks, present):
            offset = subset[:, :, None] - ghost_block[:, None, :]
            closeness = jnp.exp(-jnp.sum(offset * offset, axis=0) / (2.0 * PAIR_WIDTH * PAIR_WIDTH)) * weight
            summed = summed + jnp.sum(offset * closeness[None, :, :], axis=2)
        return summed

    return STIFFNESS * lax.map(one_group, stacked).transpose(1, 0, 2).reshape(3, particles)


def reference(fractions, velocity, drag_rate, volume, owner, element, coords, fluid):
    grid_x = fractions.shape[0]
    grid_y = fractions.shape[1]
    devices = grid_x * grid_y
    lagrange = basis_table(QUANT)
    table = fluid.reshape(devices * E_DEV, 6, 512)

    def interpolate(inputs):
        targets, local_ids, levels = inputs
        picked = table[targets * E_DEV + local_ids].astype(jnp.float32)
        first = lagrange[levels[0]]
        second = lagrange[levels[1]]
        third = lagrange[levels[2]]
        weights = (first[:, :, None, None] * second[:, None, :, None] * third[:, None, None, :]).reshape(-1, 512)
        weights = lax.optimization_barrier(weights.astype(jnp.bfloat16)).astype(jnp.float32)
        return jnp.einsum("pkn,pn->kp", picked, weights).astype(jnp.bfloat16)

    fetched = lax.map(interpolate, (owner.reshape(devices, P_DEV), element.reshape(devices, P_DEV),
                                    coords.reshape(devices, 3, P_DEV)))
    padded = jnp.pad(fractions, ((1, 1), (1, 1), (0, 0), (0, 0)))
    alive_grid = jnp.pad(jnp.ones((grid_x, grid_y), jnp.float32), 1)
    velocity_rows = velocity.reshape(devices, 3, P_DEV)
    drag_rows = drag_rate.reshape(devices, P_DEV)
    volume_rows = volume.reshape(devices, P_DEV)
    first_extent = BX + 2 * MARGIN
    second_extent = BY + 2 * MARGIN
    field = jnp.zeros((4, grid_x * BX + 2 * MARGIN, grid_y * BY + 2 * MARGIN, BINS_THIRD_AXIS), jnp.float32)
    nought = jnp.zeros((), jnp.int32)

    def per_device(field, flat):
        index_x = (flat // grid_y).astype(jnp.int32)
        index_y = (flat % grid_y).astype(jnp.int32)
        slab_x = index_x.astype(jnp.float32)
        slab_y = index_y.astype(jnp.float32)
        nearby = lax.dynamic_slice(padded, (index_x, index_y, nought, nought), (3, 3, 3, P_DEV))
        alive = lax.dynamic_slice(alive_grid, (index_x, index_y), (3, 3))
        blocks = []
        present = []
        for shift_x in (-1, 0, 1):
            for shift_y in (-1, 0, 1):
                blocks.append(place(nearby[1 + shift_x, 1 + shift_y], slab_x + shift_x, slab_y + shift_y))
                present.append(alive[1 + shift_x, 1 + shift_y])
        own = place(nearby[1, 1], slab_x, slab_y)
        pair = pair_forces(own, blocks, present)
        values = fetched[flat].astype(jnp.float32)
        force = drag_rows[flat][None, :] * (values[0:3] - velocity_rows[flat]) - volume_rows[flat][None, :] * values[3:6] + pair
        loads = jnp.concatenate([force, volume_rows[flat][None, :]], axis=0)
        scattered_loads, along_depth = window_spread(own, loads, slab_x, slab_y, (0, first_extent), (0, second_extent))
        scatter_extent = lax.optimization_barrier(scattered_loads).astype(jnp.float32)
        depth_extent = lax.optimization_barrier(along_depth).astype(jnp.float32)
        filter_cube = jnp.einsum("vtn,tl->vnl", scatter_extent, depth_extent).reshape(4, first_extent, second_extent, BINS_THIRD_AXIS)
        corner = (nought, index_x * BX, index_y * BY, nought)
        region = lax.dynamic_slice(field, corner, filter_cube.shape) + filter_cube
        return lax.dynamic_update_slice(field, region, corner), force

    field, forces = lax.scan(per_device, field, jnp.arange(devices, dtype=jnp.int32))
    bin_field = field[:, MARGIN:MARGIN + grid_x * BX, MARGIN:MARGIN + grid_y * BY] * (BX * BY * BINS_THIRD_AXIS / P_DEV)
    return forces.reshape(grid_x, grid_y, 3, P_DEV), bin_field
```

```python
import functools
import math

import jax
import jax.numpy as jnp
import numpy as np
from jax import lax
from jax.experimental import pallas as pl
from jax.experimental.pallas import tpu as pltpu
from jax.sharding import PartitionSpec as P

P_DEV = 1024
E_DEV = 32
BINS_THIRD_AXIS = 512
BX = 16
BY = 16
MARGIN = 4
QUANT = 64
CAP = 64

GLL_NODES = (
    -1.0,
    -0.8717401485096066,
    -0.5917001814331423,
    -0.2092992179024789,
    0.2092992179024789,
    0.5917001814331423,
    0.8717401485096066,
    1.0,
)
STIFFNESS = 0.5
PAIR_WIDTH = 0.3
FILTER_BINS = 3.0

f32 = jnp.float32
bf16 = jnp.bfloat16
MESH = pl.DeviceIdType.MESH

LOG2E = math.log2(math.e)
HEIGHT = BINS_THIRD_AXIS / BX
PAIR_SCALE = math.sqrt(LOG2E) / PAIR_WIDTH
DEPTH_SCALE = math.sqrt(LOG2E / 2.0) / (FILTER_BINS / BX)
EDGE_RATE = LOG2E / (2.0 * (FILTER_BINS / BX) ** 2)
FIELD_SCALE = BX * BY * BINS_THIRD_AXIS / P_DEV

STEPS = tuple((k // 3 - 1, k % 3 - 1) for k in range(9) if k != 4)
OWN = 8
ROWS_Q = 64


def basis_pieces():
    points = -1.0 + (2.0 * np.arange(QUANT) + 1.0) / QUANT
    lagrange = np.ones((QUANT, 8))
    for node_a in range(8):
        for node_b in range(8):
            if node_b != node_a:
                lagrange[:, node_a] *= (points - GLL_NODES[node_b]) / (
                    GLL_NODES[node_a] - GLL_NODES[node_b]
                )
    rest = lagrange.astype(np.float32).T
    pieces = []
    for _ in range(3):
        piece = rest.astype(bf16)
        pieces.append(piece)
        rest = rest - piece.astype(np.float32)
    pieces.append(np.zeros_like(pieces[0]))
    return np.concatenate(pieces, axis=0)


def rows_iota(shape):
    return lax.broadcasted_iota(jnp.int32, shape, 0)


def split3(x):
    high = x.astype(bf16).astype(f32)
    rest = x - high
    middle = rest.astype(bf16).astype(f32)
    low = (rest - middle).astype(bf16).astype(f32)
    return high, middle, low


def kernel(
    grid_x, grid_y,
    frac_ref, vel_ref, drag_ref, vol_ref, owner_ref, element_ref, coords_ref, table_ref, basis_ref,
    force_ref, field_ref,
    pos_send, pos_recv, req_send, req_recv, val_send, val_recv, load_send, load_recv,
    xs, fq_t, cols, feat, fp, g_ref, weights, own_val, pair_acc, wz, spread_c, spread_e, wx_ref, wy_ref,
    wx4, wy4,
    pos_ss, pos_rs, req_ss, req_rs, val_ss, val_rs, load_ss, load_rs,
):
    me_x = lax.axis_index("gx")
    me_y = lax.axis_index("gy")
    ids = []
    present = []
    for dx, dy in STEPS:
        tx, ty = me_x + dx, me_y + dy
        ids.append((lax.rem(tx + grid_x, grid_x), lax.rem(ty + grid_y, grid_y)))
        inside = (tx >= 0) & (tx < grid_x) & (ty >= 0) & (ty < grid_y)
        present.append(jnp.where(inside, 1.0, 0.0).astype(f32))

    barrier = pltpu.get_barrier_semaphore()
    for n in range(8):
        pl.semaphore_signal(barrier, inc=1, device_id=ids[n], device_id_type=MESH)

    def remote(src, dst, ss, rs, n):
        return pltpu.make_async_remote_copy(
            src_ref=src, dst_ref=dst.at[7 - n], send_sem=ss.at[n], recv_sem=rs.at[7 - n],
            device_id=ids[n], device_id_type=MESH,
        )

    pos_copies = [remote(pos_send, pos_recv, pos_ss, pos_rs, n) for n in range(8)]
    req_copies = [remote(req_send.at[n // 2], req_recv, req_ss, req_rs, n) for n in range(8)]
    val_copies = [remote(val_send.at[n // 2], val_recv, val_ss, val_rs, n) for n in range(8)]
    load_copies = [remote(load_send, load_recv, load_ss, load_rs, n) for n in range(8)]

    fz = frac_ref[2:3, :]
    z_own = fz * HEIGHT * DEPTH_SCALE

    def sum_step(i, acc):
        at = (rows_iota((64, P_DEV)) + i * 64).astype(f32)
        d = z_own - (at + 0.5) * (DEPTH_SCALE / BX)
        bumps = jnp.exp2(-(d * d))
        return acc + jnp.sum(bumps.reshape(8, 8, P_DEV), axis=0)

    partial = lax.fori_loop(0, BINS_THIRD_AXIS // 64, sum_step, jnp.zeros((8, P_DEV), f32))
    total = jnp.sum(partial, axis=0, keepdims=True)
    pos_send[0:3, :] = frac_ref[...]
    pos_send[3:4, :] = -LOG2E * jnp.log(total)

    pl.semaphore_wait(barrier, 8)
    for copy in pos_copies:
        copy.start()

    row8 = rows_iota((8, 1))
    offsets = jnp.zeros((8, 1), jnp.int32)
    for n, (dx, dy) in enumerate(STEPS):
        offsets = jnp.where(row8 == n, dx * grid_y + dy, offsets)
    delta = owner_ref[...] - (me_x * grid_y + me_y)
    chosen = jnp.where(delta == offsets, 1.0, 0.0).astype(f32)
    blocks = [chosen[:, 128 * b : 128 * b + 128] for b in range(8)]
    stacked = jnp.concatenate(blocks, axis=0).astype(bf16)
    lower = rows_iota((128, 128)) < lax.broadcasted_iota(jnp.int32, (128, 128), 1)
    earlier = jnp.dot(stacked, jnp.where(lower, 1.0, 0.0).astype(bf16), preferred_element_type=f32)
    base = (row8 * CAP).astype(f32)
    ranked = []
    for b in range(8):
        ranked.append(earlier[8 * b : 8 * b + 8] + base)
        base = base + jnp.sum(blocks[b], axis=1, keepdims=True)
    ranked = jnp.concatenate(ranked, axis=1)
    is_remote = jnp.sum(chosen, axis=0, keepdims=True)
    place = jnp.sum(chosen * ranked, axis=0, keepdims=True)
    slot = jnp.where(is_remote > 0.0, place, -1.0)
    for i in range(8):
        at = (rows_iota((64, 1)) + i * 64).astype(f32)
        g_ref[64 * i : 64 * i + 64, :] = jnp.where(slot == at, 1.0, 0.0).astype(bf16)

    xs[0:1, :] = element_ref[...].astype(f32)
    xs[1:4, :] = coords_ref[...].astype(f32)
    xs[4:8, :] = jnp.zeros((4, P_DEV), f32)
    payload = xs[...]
    payload16 = jnp.concatenate([payload, jnp.zeros((8, P_DEV), f32)], axis=0).astype(bf16)
    outgoing = lax.dot_general(
        payload16, g_ref[...], (((1,), (1,)), ((), ())), preferred_element_type=f32
    )
    for j in range(4):
        req_send[j] = outgoing[0:8, 128 * j : 128 * j + 128]
    for copy in req_copies:
        copy.start()

    def interpolate(requests):
        slots = requests.shape[1]
        levels = rows_iota((QUANT, 1)).astype(f32)
        factors = []
        for axis in range(3):
            select = jnp.where(requests[1 + axis : 2 + axis, :] == levels, 1.0, 0.0).astype(bf16)
            pieces = jnp.dot(basis_ref[...], select, preferred_element_type=f32)
            factors.append(pieces[0:8] + pieces[8:16] + pieces[16:24])
        for a in range(8):
            plane = factors[0][a : a + 1, :] * factors[1]
            for b in range(0, 8, 2):
                pair = jnp.concatenate(
                    [plane[b : b + 1, :] * factors[2], plane[b + 1 : b + 2, :] * factors[2]], axis=0
                )
                at = 64 * a + 8 * b
                weights[at : at + 16, :] = pair.astype(bf16)
        projected = jnp.dot(table_ref[...], weights[...], preferred_element_type=f32)
        element = requests[0:1, :]
        values = jnp.zeros((8, slots), f32)
        for e in range(E_DEV):
            values = values + jnp.where(element == float(e), projected[8 * e : 8 * e + 8, :], 0.0)
        return values.astype(bf16).astype(f32)

    def place_rows(dx, dy):
        row = rows_iota((8, 1))
        factor = jnp.where(row == 2, HEIGHT * PAIR_SCALE, PAIR_SCALE)
        shift = jnp.where(row == 0, dx * PAIR_SCALE, jnp.where(row == 1, dy * PAIR_SCALE, -0.5 * HEIGHT * PAIR_SCALE))
        return jnp.where(row < 3, xs[...] * factor + shift, 0.0)

    def features(m, dx, dy, weight):
        row = rows_iota((8, 1))
        where_at = place_rows(dx, dy)
        half = 0.5 * jnp.sum(where_at * where_at, axis=0, keepdims=True)
        vector = jnp.where(row == 3, -half, jnp.where(row == 4, 1.0, where_at))
        q1, q2, q3 = split3(vector)
        raw = xs[...]
        stack = jnp.concatenate([q1, q2, q1, q2, q3, q1, raw, jnp.zeros_like(raw)], axis=0)
        turned = stack.T
        fq_t[m] = turned.astype(bf16)
        cols[m] = turned[:, 48:56]
        if weight is not None:
            q1, q2, q3 = q1 * weight, q2 * weight, q3 * weight
        feat[m] = jnp.concatenate([q1, q2, q3, jnp.zeros_like(q1)], axis=0).astype(bf16)
        return where_at

    xs[0:4, :] = pos_send[...]
    xs[4:8, :] = jnp.zeros((4, P_DEV), f32)
    own_at = features(OWN, 0, 0, None)
    row8 = rows_iota((8, 1))
    half_own = 0.5 * jnp.sum(own_at * own_at, axis=0, keepdims=True)
    p1, p2, p3 = split3(jnp.where(row8 == 3, 1.0, jnp.where(row8 == 4, -half_own, own_at)))
    blank = jnp.zeros_like(p1)
    fp[...] = jnp.concatenate([p1, p1, p2, p2, p1, p3, blank, blank], axis=0).astype(bf16)

    def pair_block(m):
        exponent = jnp.dot(fq_t[m], fp[...], preferred_element_type=f32)
        closeness = jnp.exp2(exponent).astype(bf16)
        return jnp.dot(feat[m], closeness, preferred_element_type=f32)

    pair_acc[...] = pair_block(OWN)
    for half in range(2):
        own_val[:, 512 * half : 512 * half + 512] = interpolate(payload[:, 512 * half : 512 * half + 512])

    for copy in pos_copies:
        copy.wait_recv()
    for m, (dx, dy) in enumerate(STEPS):
        xs[0:4, :] = pos_recv[m]
        features(m, dx, dy, present[m])

    for copy in req_copies:
        copy.wait_recv()
    low_half = lax.broadcasted_iota(jnp.int32, (8, 128), 1) < CAP
    arrived = jnp.concatenate(
        [jnp.where(low_half, req_recv[2 * j + 1], req_recv[2 * j]) for j in range(4)], axis=1
    )
    served = interpolate(arrived)
    for j in range(4):
        val_send[j] = served[:, 128 * j : 128 * j + 128]
    for copy in val_copies:
        copy.start()

    def pair_step(m, carry):
        pair_acc[...] += pair_block(m)
        return carry

    lax.fori_loop(0, 8, pair_step, 0)

    for copy in val_copies:
        copy.wait_recv()
    returned = jnp.concatenate(
        [jnp.where(low_half, val_recv[2 * j], val_recv[2 * j + 1]) for j in range(4)], axis=1
    )
    returned16 = jnp.concatenate([returned, jnp.zeros((8, 512), f32)], axis=0).astype(bf16)
    fetched = jnp.dot(returned16, g_ref[...], preferred_element_type=f32)[0:8]
    fetched = jnp.where(is_remote > 0.0, fetched, own_val[...])
    gradient = pltpu.roll(fetched, 4, axis=0)
    sums = pair_acc[...]
    sums = sums[0:8] + sums[8:16] + sums[16:24]
    pair = (STIFFNESS / PAIR_SCALE) * (own_at * sums[4:5, :] - sums)
    xs[0:3, :] = vel_ref[...]
    volume = vol_ref[...]
    force = drag_ref[...] * (fetched - xs[...]) - volume * gradient + pair
    force_ref[...] = force[0:3]
    loads = jnp.where(row8 == 3, volume, force)
    load_send[...] = loads[0:4]
    for copy in load_copies:
        copy.start()

    def edge_rows(fraction, rows):
        d = fraction - (rows.astype(f32) + (0.5 - MARGIN)) * (1.0 / BX)
        return jnp.exp2((d * d) * (-EDGE_RATE))

    row24 = rows_iota((24, 1))
    order_y = jnp.where(row24 < 16, row24 + 4, jnp.where(row24 < 20, row24 - 16, row24))

    def all_edges(fx, fy):
        bump_x = edge_rows(fx, row24)
        bump_y = edge_rows(fy, order_y)
        scale_x = 1.0 / jnp.sum(bump_x, axis=0, keepdims=True)
        scale_y = 1.0 / jnp.sum(bump_y, axis=0, keepdims=True)
        wx_ref[...] = bump_x * scale_x
        wy_ref[...] = bump_y * scale_y

    at_z = (lax.broadcasted_iota(jnp.int32, (1, BINS_THIRD_AXIS), 1).astype(f32) + 0.5) * (DEPTH_SCALE / BX)

    def depth_rows(m):
        def depth_step(i, carry):
            r0 = pl.multiple_of(i * 64, 64)
            block = cols[m, pl.ds(r0, 64), :]
            d = block[:, 2:3] * (HEIGHT * DEPTH_SCALE) - at_z
            wz[m, pl.ds(r0, 64), :] = jnp.exp2(block[:, 3:4] - d * d).astype(bf16)
            return carry

        lax.fori_loop(0, P_DEV // 64, depth_step, 0)

    depth_rows(OWN)
    all_edges(pos_send[0:1, :], pos_send[1:2, :])

    def spread_step(a, carry):
        plane = wx_ref[pl.ds(a + MARGIN, 1), :] * wy_ref[0:16, :]
        for c in range(4):
            r0 = pl.multiple_of((c * 16 + a) * 16, 16)
            spread_c[pl.ds(r0, 16), :] = (plane * (load_send[c : c + 1, :] * FIELD_SCALE)).astype(bf16)
        return carry

    lax.fori_loop(0, 16, spread_step, 0)

    for c in range(4):
        part = jnp.dot(spread_c[256 * c : 256 * c + 256, :], wz[OWN], preferred_element_type=f32)
        field_ref[c] = part.reshape(16, 16, BINS_THIRD_AXIS)

    def neighbour_depth(m, carry):
        depth_rows(m)
        return carry

    lax.fori_loop(0, 8, neighbour_depth, 0)

    for copy in load_copies:
        copy.wait_recv()
    for m, (dx, dy) in enumerate(STEPS):
        all_edges(pos_recv[m, 0:1, :], pos_recv[m, 1:2, :])
        loads_m = [load_recv[m, c : c + 1, :] * (FIELD_SCALE * present[m]) for c in range(4)]
        source_x = {-1: 20, 0: 4, 1: 0}[dx]
        target_x = {-1: 0, 0: 0, 1: 12}[dx]
        count_x = 16 if dx == 0 else 4
        if dy == 0:
            for a in range(count_x):
                plane = wx_ref[source_x + a : source_x + a + 1, :] * wy_ref[0:16, :]
                for c in range(4):
                    r0 = (c * count_x + a) * 16
                    spread_e[r0 : r0 + 16, :] = (plane * loads_m[c]).astype(bf16)
            part = jnp.dot(spread_e[...], wz[m], preferred_element_type=f32)
            for c in range(4):
                field_ref[c, target_x : target_x + 4] += part[64 * c : 64 * c + 64].reshape(4, 16, BINS_THIRD_AXIS)
        else:
            first = 20 if dy == -1 else 16
            target_y = 0 if dy == -1 else 12
            wy4[0:4, :] = wy_ref[first : first + 4, :]
            wy4[4:8, :] = wy_ref[first : first + 4, :]
            top = rows_iota((8, 1)) < 4
            for a in range(0, count_x, 4):
                planes = []
                for pair_at in (a, a + 2):
                    s = source_x + pair_at
                    planes.append(jnp.where(top, wx_ref[s : s + 1, :], wx_ref[s + 1 : s + 2, :]) * wy4[...])
                plane = jnp.concatenate(planes, axis=0)
                for c in range(4):
                    r0 = (c * count_x + a) * 4
                    spread_e[r0 : r0 + 16, :] = (plane * loads_m[c]).astype(bf16)
            used = 16 * count_x
            part = jnp.dot(spread_e[0:used, :], wz[m], preferred_element_type=f32)
            for c in range(4):
                for a in range(count_x):
                    r0 = (c * count_x + a) * 4
                    field_ref[c, target_x + a, target_y : target_y + 4, :] += part[r0 : r0 + 4, :]

    for copy in pos_copies + req_copies + val_copies + load_copies:
        copy.wait_send()


def body(fractions, velocity, drag_rate, volume, owner, element, coords, fluid):
    grid_x = lax.axis_size("gx")
    grid_y = lax.axis_size("gy")
    nodes = fluid.reshape(E_DEV, 6, 512)
    nothing = jnp.zeros((E_DEV, 1, 512), bf16)
    table = jnp.concatenate([nodes[:, 0:3], nothing, nodes[:, 3:6], nothing], axis=1).reshape(256, 512)
    vmem = pl.BlockSpec(memory_space=pltpu.VMEM)
    dma = pltpu.SemaphoreType.DMA((8,))
    force, field = pl.pallas_call(
        functools.partial(kernel, grid_x, grid_y),
        out_shape=(
            jax.ShapeDtypeStruct((3, P_DEV), f32),
            jax.ShapeDtypeStruct((4, BX, BY, BINS_THIRD_AXIS), f32),
        ),
        in_specs=[vmem] * 9,
        out_specs=(vmem, vmem),
        scratch_shapes=[
            pltpu.VMEM((4, P_DEV), f32),
            pltpu.VMEM((8, 4, P_DEV), f32),
            pltpu.VMEM((4, 8, 128), f32),
            pltpu.VMEM((8, 8, 128), f32),
            pltpu.VMEM((4, 8, 128), f32),
            pltpu.VMEM((8, 8, 128), f32),
            pltpu.VMEM((4, P_DEV), f32),
            pltpu.VMEM((8, 4, P_DEV), f32),
            pltpu.VMEM((8, P_DEV), f32),
            pltpu.VMEM((9, P_DEV, ROWS_Q), bf16),
            pltpu.VMEM((9, P_DEV, 8), f32),
            pltpu.VMEM((9, 32, P_DEV), bf16),
            pltpu.VMEM((ROWS_Q, P_DEV), bf16),
            pltpu.VMEM((8 * CAP, P_DEV), bf16),
            pltpu.VMEM((512, 512), bf16),
            pltpu.VMEM((8, P_DEV), f32),
            pltpu.VMEM((32, P_DEV), f32),
            pltpu.VMEM((9, P_DEV, BINS_THIRD_AXIS), bf16),
            pltpu.VMEM((1024, P_DEV), bf16),
            pltpu.VMEM((256, P_DEV), bf16),
            pltpu.VMEM((24, P_DEV), f32),
            pltpu.VMEM((24, P_DEV), f32),
            pltpu.VMEM((24, P_DEV), f32),
            pltpu.VMEM((8, P_DEV), f32),
        ]
        + [dma] * 8,
        compiler_params=pltpu.CompilerParams(
            collective_id=0, has_side_effects=True, vmem_limit_bytes=50 * 1024 * 1024
        ),
        name="particle_step",
    )(
        fractions.reshape(3, P_DEV),
        velocity.reshape(3, P_DEV),
        drag_rate.reshape(1, P_DEV),
        volume.reshape(1, P_DEV),
        owner.reshape(1, P_DEV),
        element.reshape(1, P_DEV),
        coords.reshape(3, P_DEV),
        table,
        jnp.asarray(basis_pieces()),
    )
    return force.reshape(1, 1, 3, P_DEV), field


def solution(mesh):
    return jax.shard_map(
        body,
        mesh=mesh,
        in_specs=(
            P("gx", "gy", None, None),
            P("gx", "gy", None, None),
            P("gx", "gy", None),
            P("gx", "gy", None),
            P("gx", "gy", None, None),
            P("gx", "gy", None),
            P("gx", "gy", None, None),
            P("gx", "gy", None, None, None),
        ),
        out_specs=(P("gx", "gy", None, None), P(None, "gx", "gy", None)),
        check_vma=False,
    )
```

```python
import functools
import math

import jax
import jax.numpy as jnp
import numpy as np
from jax import lax
from jax.experimental import pallas as pl
from jax.experimental.pallas import tpu as pltpu
from jax.sharding import PartitionSpec as P

P_DEV = 1024
E_DEV = 32
BINS_THIRD_AXIS = 512
BX = 16
BY = 16
MARGIN = 4
QUANT = 64
CAP = 64

GLL_NODES = (
    -1.0,
    -0.8717401485096066,
    -0.5917001814331423,
    -0.2092992179024789,
    0.2092992179024789,
    0.5917001814331423,
    0.8717401485096066,
    1.0,
)
STIFFNESS = 0.5
PAIR_WIDTH = 0.3
FILTER_BINS = 3.0

f32 = jnp.float32
bf16 = jnp.bfloat16
MESH = pl.DeviceIdType.MESH

LOG2E = math.log2(math.e)
HEIGHT = BINS_THIRD_AXIS / BX
PAIR_SCALE = math.sqrt(LOG2E) / PAIR_WIDTH
DEPTH_SCALE = math.sqrt(LOG2E / 2.0) / (FILTER_BINS / BX)
EDGE_RATE = LOG2E / (2.0 * (FILTER_BINS / BX) ** 2)
FIELD_SCALE = BX * BY * BINS_THIRD_AXIS / P_DEV

STEPS = tuple((k // 3 - 1, k % 3 - 1) for k in range(9) if k != 4)
OWN = 8
ROWS_Q = 64


def basis_pieces():
    points = -1.0 + (2.0 * np.arange(QUANT) + 1.0) / QUANT
    lagrange = np.ones((QUANT, 8))
    for node_a in range(8):
        for node_b in range(8):
            if node_b != node_a:
                lagrange[:, node_a] *= (points - GLL_NODES[node_b]) / (
                    GLL_NODES[node_a] - GLL_NODES[node_b]
                )
    rest = lagrange.astype(np.float32).T
    pieces = []
    for _ in range(3):
        piece = rest.astype(bf16)
        pieces.append(piece)
        rest = rest - piece.astype(np.float32)
    pieces.append(np.zeros_like(pieces[0]))
    return np.concatenate(pieces, axis=0)


def depth_pieces():
    centres = ((np.arange(BINS_THIRD_AXIS) + 0.5) / BX - 0.5 * HEIGHT) * DEPTH_SCALE
    rows = np.zeros((8, BINS_THIRD_AXIS))
    rows[2] = 2.0 * centres * (DEPTH_SCALE / PAIR_SCALE)
    rows[4] = -centres * centres
    pieces = []
    for _ in range(3):
        piece = rows.astype(bf16)
        pieces.append(piece)
        rows = rows - piece.astype(np.float64)
    first, second, third = pieces
    last = np.zeros((16, BINS_THIRD_AXIS))
    last[0:3] = 1.0
    return np.concatenate([first, first, second, second, first, third, last.astype(bf16)], axis=0)


def rows_iota(shape):
    return lax.broadcasted_iota(jnp.int32, shape, 0)


def split3(x):
    high = x.astype(bf16).astype(f32)
    rest = x - high
    middle = rest.astype(bf16).astype(f32)
    low = (rest - middle).astype(bf16).astype(f32)
    return high, middle, low


def kernel(
    grid_x, grid_y,
    frac_in, vel_in, drag_in, vol_in, owner_in, element_in, coords_in, table_in, basis_in, depth_in,
    force_out, field_out,
    force_ref, field_ref,
    frac_ref, vel_ref, drag_ref, vol_ref, owner_ref, element_ref, coords_ref, table_ref, basis_ref, depth_ref,
    pos_send, pos_recv, req_send, req_recv, val_send, val_recv, load_send, load_recv,
    xs, fq_t, feat, fp, g_ref, weights, own_val, pair_acc, wz, spread_c, spread_e, wx_ref, wy_ref,
    wx4, wy4,
    in_ss, out_ss, pos_ss, pos_rs, req_ss, req_rs, val_ss, val_rs, load_ss, load_rs,
):
    inputs = (
        (frac_in, frac_ref), (owner_in, owner_ref), (element_in, element_ref), (coords_in, coords_ref),
        (basis_in, basis_ref), (table_in, table_ref), (vel_in, vel_ref), (drag_in, drag_ref), (vol_in, vol_ref),
        (depth_in, depth_ref),
    )
    loads_in = [pltpu.make_async_copy(src, dst, in_ss.at[k]) for k, (src, dst) in enumerate(inputs)]
    for copy in loads_in:
        copy.start()

    me_x = lax.axis_index("gx")
    me_y = lax.axis_index("gy")
    ids = []
    present = []
    for dx, dy in STEPS:
        tx, ty = me_x + dx, me_y + dy
        ids.append((lax.rem(tx + grid_x, grid_x), lax.rem(ty + grid_y, grid_y)))
        inside = (tx >= 0) & (tx < grid_x) & (ty >= 0) & (ty < grid_y)
        present.append(jnp.where(inside, 1.0, 0.0).astype(f32))

    barrier = pltpu.get_barrier_semaphore()
    for n in range(8):
        pl.semaphore_signal(barrier, inc=1, device_id=ids[n], device_id_type=MESH)

    def remote(src, dst, ss, rs, n):
        return pltpu.make_async_remote_copy(
            src_ref=src, dst_ref=dst.at[7 - n], send_sem=ss.at[n], recv_sem=rs.at[7 - n],
            device_id=ids[n], device_id_type=MESH,
        )

    pos_copies = [remote(pos_send, pos_recv, pos_ss, pos_rs, n) for n in range(8)]
    req_copies = [remote(req_send.at[n // 2], req_recv, req_ss, req_rs, n) for n in range(8)]
    val_copies = [remote(val_send.at[n // 2], val_recv, val_ss, val_rs, n) for n in range(8)]
    load_copies = [remote(load_send, load_recv, load_ss, load_rs, n) for n in range(8)]

    loads_in[0].wait()
    fz = frac_ref[2]
    z_own = fz * HEIGHT * DEPTH_SCALE

    def sum_step(i, acc):
        at = (rows_iota((64, P_DEV)) + i * 64).astype(f32)
        d = z_own - (at + 0.5) * (DEPTH_SCALE / BX)
        bumps = jnp.exp2(-(d * d))
        return acc + jnp.sum(bumps.reshape(8, 8, P_DEV), axis=0)

    partial = lax.fori_loop(0, BINS_THIRD_AXIS // 64, sum_step, jnp.zeros((8, P_DEV), f32))
    total = jnp.sum(partial, axis=0, keepdims=True)
    for d in range(3):
        pos_send[d : d + 1, :] = frac_ref[d]
    pos_send[3:4, :] = -LOG2E * jnp.log(total)

    pl.semaphore_wait(barrier, 8)
    for copy in pos_copies:
        copy.start()

    for copy in loads_in[1:]:
        copy.wait()
    row8 = rows_iota((8, 1))
    offsets = jnp.zeros((8, 1), jnp.int32)
    for n, (dx, dy) in enumerate(STEPS):
        offsets = jnp.where(row8 == n, dx * grid_y + dy, offsets)
    delta = owner_ref[...] - (me_x * grid_y + me_y)
    chosen = jnp.where(delta == offsets, 1.0, 0.0).astype(f32)
    blocks = [chosen[:, 128 * b : 128 * b + 128] for b in range(8)]
    stacked = jnp.concatenate(blocks, axis=0).astype(bf16)
    lower = rows_iota((128, 128)) < lax.broadcasted_iota(jnp.int32, (128, 128), 1)
    earlier = jnp.dot(stacked, jnp.where(lower, 1.0, 0.0).astype(bf16), preferred_element_type=f32)
    base = (row8 * CAP).astype(f32)
    ranked = []
    for b in range(8):
        ranked.append(earlier[8 * b : 8 * b + 8] + base)
        base = base + jnp.sum(blocks[b], axis=1, keepdims=True)
    ranked = jnp.concatenate(ranked, axis=1)
    is_remote = jnp.sum(chosen, axis=0, keepdims=True)
    place = jnp.sum(chosen * ranked, axis=0, keepdims=True)
    slot = jnp.where(is_remote > 0.0, place, -1.0)
    for i in range(8):
        at = (rows_iota((64, 1)) + i * 64).astype(f32)
        g_ref[64 * i : 64 * i + 64, :] = jnp.where(slot == at, 1.0, 0.0).astype(bf16)

    xs[0:1, :] = element_ref[...].astype(f32)
    for d in range(3):
        xs[1 + d : 2 + d, :] = coords_ref[d].astype(f32)
    xs[4:8, :] = jnp.zeros((4, P_DEV), f32)
    payload = xs[...]
    payload16 = jnp.concatenate([payload, jnp.zeros((8, P_DEV), f32)], axis=0).astype(bf16)
    outgoing = lax.dot_general(
        payload16, g_ref[...], (((1,), (1,)), ((), ())), preferred_element_type=f32
    )
    for j in range(4):
        req_send[j] = outgoing[0:8, 128 * j : 128 * j + 128]
    for copy in req_copies:
        copy.start()

    def interpolate(requests):
        slots = requests.shape[1]
        levels = rows_iota((QUANT, 1)).astype(f32)
        factors = []
        for axis in range(3):
            select = jnp.where(requests[1 + axis : 2 + axis, :] == levels, 1.0, 0.0).astype(bf16)
            pieces = jnp.dot(basis_ref[...], select, preferred_element_type=f32)
            factors.append(pieces[0:8] + pieces[8:16] + pieces[16:24])
        for a in range(8):
            plane = factors[0][a : a + 1, :] * factors[1]
            for b in range(0, 8, 2):
                pair = jnp.concatenate(
                    [plane[b : b + 1, :] * factors[2], plane[b + 1 : b + 2, :] * factors[2]], axis=0
                )
                at = 64 * a + 8 * b
                weights[at : at + 16, :] = pair.astype(bf16)
        projected = jnp.dot(table_ref[...], weights[...], preferred_element_type=f32)
        mine = requests[0:1, :] == rows_iota((E_DEV, 1)).astype(f32)
        values = [
            jnp.sum(jnp.where(mine, projected[E_DEV * k : E_DEV * k + E_DEV, :], 0.0), axis=0, keepdims=True)
            for k in range(6)
        ]
        values = jnp.concatenate(values + [jnp.zeros((2, slots), f32)], axis=0)
        return values.astype(bf16).astype(f32)

    def place_rows(dx, dy):
        row = rows_iota((8, 1))
        factor = jnp.where(row == 2, HEIGHT * PAIR_SCALE, PAIR_SCALE)
        shift = jnp.where(row == 0, dx * PAIR_SCALE, jnp.where(row == 1, dy * PAIR_SCALE, -0.5 * HEIGHT * PAIR_SCALE))
        return jnp.where(row < 3, xs[...] * factor + shift, 0.0)

    def features(m, dx, dy, weight):
        row = rows_iota((8, 1))
        where_at = place_rows(dx, dy)
        half = 0.5 * jnp.sum(where_at * where_at, axis=0, keepdims=True)
        vector = jnp.where(row == 3, -half, jnp.where(row == 4, 1.0, where_at))
        q1, q2, q3 = split3(vector)
        depth = where_at[2:3, :] * (DEPTH_SCALE / PAIR_SCALE)
        h1, h2, h3 = split3(xs[3:4, :] - depth * depth)
        level = jnp.where(row == 0, h1, jnp.where(row == 1, h2, jnp.where(row == 2, h3, 0.0)))
        stack = jnp.concatenate([q1, q2, q1, q2, q3, q1, level, jnp.zeros_like(level)], axis=0)
        fq_t[m] = stack.T.astype(bf16)
        if weight is not None:
            q1, q2, q3 = q1 * weight, q2 * weight, q3 * weight
        feat[m] = jnp.concatenate([q1, q2, q3, jnp.zeros_like(q1)], axis=0).astype(bf16)
        return where_at

    xs[0:4, :] = pos_send[...]
    xs[4:8, :] = jnp.zeros((4, P_DEV), f32)
    own_at = features(OWN, 0, 0, None)
    row8 = rows_iota((8, 1))
    half_own = 0.5 * jnp.sum(own_at * own_at, axis=0, keepdims=True)
    p1, p2, p3 = split3(jnp.where(row8 == 3, 1.0, jnp.where(row8 == 4, -half_own, own_at)))
    blank = jnp.zeros_like(p1)
    fp[...] = jnp.concatenate([p1, p1, p2, p2, p1, p3, blank, blank], axis=0).astype(bf16)

    def pair_block(m):
        exponent = jnp.dot(fq_t[m], fp[...], preferred_element_type=f32)
        closeness = jnp.exp2(exponent).astype(bf16)
        return jnp.dot(feat[m], closeness, preferred_element_type=f32)

    def edge_rows(fraction, rows):
        d = fraction - (rows.astype(f32) + (0.5 - MARGIN)) * (1.0 / BX)
        return jnp.exp2((d * d) * (-EDGE_RATE))

    row24 = rows_iota((24, 1))
    order_y = jnp.where(row24 < 16, row24 + 4, jnp.where(row24 < 20, row24 - 16, row24))

    def all_edges(fx, fy):
        bump_x = edge_rows(fx, row24)
        bump_y = edge_rows(fy, order_y)
        scale_x = 1.0 / jnp.sum(bump_x, axis=0, keepdims=True)
        scale_y = 1.0 / jnp.sum(bump_y, axis=0, keepdims=True)
        wx_ref[...] = bump_x * scale_x
        wy_ref[...] = bump_y * scale_y

    def depth_rows(m):
        exponent = jnp.dot(fq_t[m], depth_ref[...], preferred_element_type=f32)
        wz[m] = jnp.exp2(exponent).astype(bf16)

    pair_acc[...] = pair_block(OWN)
    for half in range(2):
        own_val[:, 512 * half : 512 * half + 512] = interpolate(payload[:, 512 * half : 512 * half + 512])
    all_edges(pos_send[0:1, :], pos_send[1:2, :])
    depth_rows(OWN)

    def arrive(m):
        pos_copies[7 - m].wait_recv()

    def neighbour_features(m):
        xs[0:4, :] = pos_recv[m]
        features(m, STEPS[m][0], STEPS[m][1], present[m])

    for m in (3, 4):
        arrive(m)
    for m in (3, 4):
        neighbour_features(m)
    pair_acc[...] += pair_block(3) + pair_block(4)
    for m in (0, 1, 2, 5, 6, 7):
        arrive(m)
    for m in (0, 1, 2, 5, 6, 7):
        neighbour_features(m)

    for copy in req_copies:
        copy.wait_recv()
    low_half = lax.broadcasted_iota(jnp.int32, (8, 128), 1) < CAP
    arrived = jnp.concatenate(
        [jnp.where(low_half, req_recv[2 * j + 1], req_recv[2 * j]) for j in range(4)], axis=1
    )
    served = interpolate(arrived)
    for j in range(4):
        val_send[j] = served[:, 128 * j : 128 * j + 128]
    for copy in val_copies:
        copy.start()

    def pair_step(m, carry):
        pair_acc[...] += pair_block(m) + pair_block(m + 5)
        return carry

    lax.fori_loop(0, 3, pair_step, 0)

    for copy in val_copies:
        copy.wait_recv()
    returned = jnp.concatenate(
        [jnp.where(low_half, val_recv[2 * j], val_recv[2 * j + 1]) for j in range(4)], axis=1
    )
    returned16 = jnp.concatenate([returned, jnp.zeros((8, 512), f32)], axis=0).astype(bf16)
    fetched = jnp.dot(returned16, g_ref[...], preferred_element_type=f32)[0:8]
    fetched = jnp.where(is_remote > 0.0, fetched, own_val[...])
    gradient = pltpu.roll(fetched, 5, axis=0)
    sums = pair_acc[...]
    sums = sums[0:8] + sums[8:16] + sums[16:24]
    pair = (STIFFNESS / PAIR_SCALE) * (own_at * sums[4:5, :] - sums)
    for d in range(3):
        xs[d : d + 1, :] = vel_ref[d]
    volume = vol_ref[...]
    force = drag_ref[...] * (fetched - xs[...]) - volume * gradient + pair
    for d in range(3):
        force_ref[d] = force[d : d + 1]
    force_copy = pltpu.make_async_copy(force_ref, force_out, out_ss.at[0])
    force_copy.start()
    loads = jnp.where(row8 == 3, volume, force)
    load_send[...] = loads[0:4]
    for copy in load_copies:
        copy.start()

    def spread_step(a, carry):
        plane = wx_ref[pl.ds(a + MARGIN, 1), :] * wy_ref[0:16, :]
        for c in range(4):
            r0 = pl.multiple_of((c * 16 + a) * 16, 16)
            spread_c[pl.ds(r0, 16), :] = (plane * (load_send[c : c + 1, :] * FIELD_SCALE)).astype(bf16)
        return carry

    lax.fori_loop(0, 16, spread_step, 0)

    for c in range(4):
        part = jnp.dot(spread_c[256 * c : 256 * c + 256, :], wz[OWN], preferred_element_type=f32)
        field_ref[c] = part.reshape(16, 16, BINS_THIRD_AXIS)

    def neighbour_depth(m, carry):
        depth_rows(2 * m)
        depth_rows(2 * m + 1)
        return carry

    lax.fori_loop(0, 4, neighbour_depth, 0)

    for copy in load_copies:
        copy.wait_recv()
    out_copies = [force_copy]

    def write_slabs(first, count, k):
        part = pl.ds(first, count)
        copy = pltpu.make_async_copy(field_ref.at[:, part], field_out.at[:, part], out_ss.at[k])
        copy.start()
        out_copies.append(copy)

    for m in (3, 4, 0, 1, 2, 5, 6, 7):
        dx, dy = STEPS[m]
        all_edges(pos_recv[m, 0:1, :], pos_recv[m, 1:2, :])
        loads_m = [load_recv[m, c : c + 1, :] * (FIELD_SCALE * present[m]) for c in range(4)]
        source_x = {-1: 20, 0: 4, 1: 0}[dx]
        target_x = {-1: 0, 0: 0, 1: 12}[dx]
        count_x = 16 if dx == 0 else 4
        if dy == 0:
            for a in range(count_x):
                plane = wx_ref[source_x + a : source_x + a + 1, :] * wy_ref[0:16, :]
                for c in range(4):
                    r0 = (c * count_x + a) * 16
                    spread_e[r0 : r0 + 16, :] = (plane * loads_m[c]).astype(bf16)
            part = jnp.dot(spread_e[...], wz[m], preferred_element_type=f32)
            for c in range(4):
                field_ref[c, target_x : target_x + 4] += part[64 * c : 64 * c + 64].reshape(4, 16, BINS_THIRD_AXIS)
        else:
            first = 20 if dy == -1 else 16
            target_y = 0 if dy == -1 else 12
            wy4[0:4, :] = wy_ref[first : first + 4, :]
            wy4[4:8, :] = wy_ref[first : first + 4, :]
            top = rows_iota((8, 1)) < 4
            for a in range(0, count_x, 4):
                planes = []
                for pair_at in (a, a + 2):
                    s = source_x + pair_at
                    planes.append(jnp.where(top, wx_ref[s : s + 1, :], wx_ref[s + 1 : s + 2, :]) * wy4[...])
                plane = jnp.concatenate(planes, axis=0)
                for c in range(4):
                    r0 = (c * count_x + a) * 4
                    spread_e[r0 : r0 + 16, :] = (plane * loads_m[c]).astype(bf16)
            used = 16 * count_x
            part = jnp.dot(spread_e[0:used, :], wz[m], preferred_element_type=f32)
            for c in range(4):
                for a in range(count_x):
                    r0 = (c * count_x + a) * 4
                    field_ref[c, target_x + a, target_y : target_y + 4, :] += part[r0 : r0 + 4, :]

        if m == 4:
            write_slabs(4, 8, 1)
        if m == 2:
            write_slabs(0, 4, 2)
    write_slabs(12, 4, 3)
    for copy in out_copies:
        copy.wait()
    for copy in pos_copies + req_copies + val_copies + load_copies:
        copy.wait_send()


def publish(force_in, field_in, force_out, field_out, force_v, field_v, in_sems, out_sems):
    pairs = [(force_in, force_v, force_out)]
    for c in range(4):
        for k in range(4):
            part = pl.ds(4 * k, 4)
            pairs.append((field_in.at[c, part], field_v.at[c, part], field_out.at[c, part]))
    ins = [pltpu.make_async_copy(a, v, in_sems.at[i]) for i, (a, v, o) in enumerate(pairs)]
    outs = [pltpu.make_async_copy(v, o, out_sems.at[i]) for i, (a, v, o) in enumerate(pairs)]
    for copy in ins:
        copy.start()
    for first, second in zip(ins, outs):
        first.wait()
        second.start()
    for copy in outs:
        copy.wait()


def body(fractions, velocity, drag_rate, volume, owner, element, coords, fluid):
    grid_x = lax.axis_size("gx")
    grid_y = lax.axis_size("gy")
    table = jnp.transpose(fluid.reshape(E_DEV, 6, 512), (1, 0, 2)).reshape(E_DEV * 6, 512)
    hbm = pl.BlockSpec(memory_space=pl.ANY)
    dma = pltpu.SemaphoreType.DMA((8,))
    force, field = pl.pallas_call(
        functools.partial(kernel, grid_x, grid_y),
        out_shape=(
            jax.ShapeDtypeStruct((3, 1, P_DEV), f32),
            jax.ShapeDtypeStruct((4, BX, BY, BINS_THIRD_AXIS), f32),
        ),
        in_specs=[hbm] * 10,
        out_specs=(hbm, hbm),
        scratch_shapes=[
            pltpu.VMEM((3, 1, P_DEV), f32),
            pltpu.VMEM((4, BX, BY, BINS_THIRD_AXIS), f32),
            pltpu.VMEM((3, 1, P_DEV), f32),
            pltpu.VMEM((3, 1, P_DEV), f32),
            pltpu.VMEM((1, P_DEV), f32),
            pltpu.VMEM((1, P_DEV), f32),
            pltpu.VMEM((1, P_DEV), jnp.int32),
            pltpu.VMEM((1, P_DEV), jnp.int32),
            pltpu.VMEM((3, 1, P_DEV), jnp.int32),
            pltpu.VMEM((6 * E_DEV, 512), bf16),
            pltpu.VMEM((32, QUANT), bf16),
            pltpu.VMEM((ROWS_Q, BINS_THIRD_AXIS), bf16),
            pltpu.VMEM((4, P_DEV), f32),
            pltpu.VMEM((8, 4, P_DEV), f32),
            pltpu.VMEM((4, 8, 128), f32),
            pltpu.VMEM((8, 8, 128), f32),
            pltpu.VMEM((4, 8, 128), f32),
            pltpu.VMEM((8, 8, 128), f32),
            pltpu.VMEM((4, P_DEV), f32),
            pltpu.VMEM((8, 4, P_DEV), f32),
            pltpu.VMEM((8, P_DEV), f32),
            pltpu.VMEM((9, P_DEV, ROWS_Q), bf16),
            pltpu.VMEM((9, 32, P_DEV), bf16),
            pltpu.VMEM((ROWS_Q, P_DEV), bf16),
            pltpu.VMEM((8 * CAP, P_DEV), bf16),
            pltpu.VMEM((512, 512), bf16),
            pltpu.VMEM((8, P_DEV), f32),
            pltpu.VMEM((32, P_DEV), f32),
            pltpu.VMEM((9, P_DEV, BINS_THIRD_AXIS), bf16),
            pltpu.VMEM((1024, P_DEV), bf16),
            pltpu.VMEM((256, P_DEV), bf16),
            pltpu.VMEM((24, P_DEV), f32),
            pltpu.VMEM((24, P_DEV), f32),
            pltpu.VMEM((24, P_DEV), f32),
            pltpu.VMEM((8, P_DEV), f32),
        ]
        + [pltpu.SemaphoreType.DMA((10,)), pltpu.SemaphoreType.DMA((4,))] + [dma] * 8,
        compiler_params=pltpu.CompilerParams(
            collective_id=0, has_side_effects=True, vmem_limit_bytes=60 * 1024 * 1024
        ),
        name="particle_step",
    )(
        fractions.reshape(3, 1, P_DEV),
        velocity.reshape(3, 1, P_DEV),
        drag_rate.reshape(1, P_DEV),
        volume.reshape(1, P_DEV),
        owner.reshape(1, P_DEV),
        element.reshape(1, P_DEV),
        coords.reshape(3, 1, P_DEV),
        table,
        jnp.asarray(basis_pieces()),
        jnp.asarray(depth_pieces()),
    )
    force, field = pl.pallas_call(
        publish,
        out_shape=(
            jax.ShapeDtypeStruct((3, 1, P_DEV), f32),
            jax.ShapeDtypeStruct((4, BX, BY, BINS_THIRD_AXIS), f32),
        ),
        in_specs=[hbm] * 2,
        out_specs=(hbm, hbm),
        scratch_shapes=[
            pltpu.VMEM((3, 1, P_DEV), f32),
            pltpu.VMEM((4, BX, BY, BINS_THIRD_AXIS), f32),
            pltpu.SemaphoreType.DMA((17,)),
            pltpu.SemaphoreType.DMA((17,)),
        ],
        compiler_params=pltpu.CompilerParams(vmem_limit_bytes=60 * 1024 * 1024),
        name="publish",
    )(force, field)
    return force.reshape(1, 1, 3, P_DEV), field


def solution(mesh):
    return jax.shard_map(
        body,
        mesh=mesh,
        in_specs=(
            P("gx", "gy", None, None),
            P("gx", "gy", None, None),
            P("gx", "gy", None),
            P("gx", "gy", None),
            P("gx", "gy", None, None),
            P("gx", "gy", None),
            P("gx", "gy", None, None),
            P("gx", "gy", None, None, None),
        ),
        out_specs=(P("gx", "gy", None, None), P(None, "gx", "gy", None)),
        check_vma=False,
    )
```

```python
import functools
import math

import jax
import jax.numpy as jnp
import numpy as np
from jax import lax
from jax.experimental import pallas as pl
from jax.experimental.pallas import tpu as pltpu
from jax.sharding import PartitionSpec as P

P_DEV = 1024
E_DEV = 32
BINS_THIRD_AXIS = 512
BX = 16
BY = 16
MARGIN = 4
QUANT = 64
CAP = 64

GLL_NODES = (
    -1.0,
    -0.8717401485096066,
    -0.5917001814331423,
    -0.2092992179024789,
    0.2092992179024789,
    0.5917001814331423,
    0.8717401485096066,
    1.0,
)
STIFFNESS = 0.5
PAIR_WIDTH = 0.3
FILTER_BINS = 3.0

f32 = jnp.float32
bf16 = jnp.bfloat16
MESH = pl.DeviceIdType.MESH

LOG2E = math.log2(math.e)
HEIGHT = BINS_THIRD_AXIS / BX
PAIR_SCALE = math.sqrt(LOG2E) / PAIR_WIDTH
DEPTH_SCALE = math.sqrt(LOG2E / 2.0) / (FILTER_BINS / BX)
EDGE_RATE = LOG2E / (2.0 * (FILTER_BINS / BX) ** 2)
FIELD_SCALE = BX * BY * BINS_THIRD_AXIS / P_DEV

STEPS = tuple((k // 3 - 1, k % 3 - 1) for k in range(9) if k != 4)
OWN = 8
ROWS_Q = 64


def basis_pieces():
    points = -1.0 + (2.0 * np.arange(QUANT) + 1.0) / QUANT
    lagrange = np.ones((QUANT, 8))
    for node_a in range(8):
        for node_b in range(8):
            if node_b != node_a:
                lagrange[:, node_a] *= (points - GLL_NODES[node_b]) / (
                    GLL_NODES[node_a] - GLL_NODES[node_b]
                )
    rest = lagrange.astype(np.float32).T
    pieces = []
    for _ in range(3):
        piece = rest.astype(bf16)
        pieces.append(piece)
        rest = rest - piece.astype(np.float32)
    pieces.append(np.zeros_like(pieces[0]))
    return np.concatenate(pieces, axis=0)


def depth_pieces():
    centres = ((np.arange(BINS_THIRD_AXIS) + 0.5) / BX - 0.5 * HEIGHT) * DEPTH_SCALE
    rows = np.zeros((8, BINS_THIRD_AXIS))
    rows[2] = 2.0 * centres * (DEPTH_SCALE / PAIR_SCALE)
    rows[4] = -centres * centres
    pieces = []
    for _ in range(3):
        piece = rows.astype(bf16)
        pieces.append(piece)
        rows = rows - piece.astype(np.float64)
    first, second, third = pieces
    last = np.zeros((16, BINS_THIRD_AXIS))
    last[0:3] = 1.0
    return np.concatenate([first, first, second, second, first, third, last.astype(bf16)], axis=0)


def rows_iota(shape):
    return lax.broadcasted_iota(jnp.int32, shape, 0)


def split3(x):
    high = x.astype(bf16).astype(f32)
    rest = x - high
    middle = rest.astype(bf16).astype(f32)
    low = (rest - middle).astype(bf16).astype(f32)
    return high, middle, low


def kernel(
    grid_x, grid_y,
    frac_in, vel_in, drag_in, vol_in, owner_in, element_in, coords_in, table_in, basis_in, depth_in,
    force_out, field_out,
    force_ref, field_ref,
    frac_ref, vel_ref, drag_ref, vol_ref, owner_ref, element_ref, coords_ref, table_ref, basis_ref, depth_ref,
    pos_send, pos_recv, req_send, req_recv, val_send, val_recv, load_send, load_recv,
    xs, fq_t, feat, fp, g_ref, weights, own_val, pair_acc, wz, spread_c, spread_e, wx_ref, wy_ref,
    wx4, wy4,
    in_ss, out_ss, pos_ss, pos_rs, req_ss, req_rs, val_ss, val_rs, load_ss, load_rs,
):
    inputs = (
        (frac_in, frac_ref), (owner_in, owner_ref), (element_in, element_ref), (coords_in, coords_ref),
        (basis_in, basis_ref), (table_in, table_ref), (vel_in, vel_ref), (drag_in, drag_ref), (vol_in, vol_ref),
        (depth_in, depth_ref),
    )
    loads_in = [pltpu.make_async_copy(src, dst, in_ss.at[k]) for k, (src, dst) in enumerate(inputs)]
    for copy in loads_in:
        copy.start()

    me_x = lax.axis_index("gx")
    me_y = lax.axis_index("gy")
    ids = []
    present = []
    inside = []
    for dx, dy in STEPS:
        tx, ty = me_x + dx, me_y + dy
        ids.append((lax.rem(tx + grid_x, grid_x), lax.rem(ty + grid_y, grid_y)))
        within = (tx >= 0) & (tx < grid_x) & (ty >= 0) & (ty < grid_y)
        inside.append(within)
        present.append(jnp.where(within, 1.0, 0.0).astype(f32))
    groups = ((None, (3, 4)), (me_x > 0, (0, 1, 2)), (me_x < grid_x - 1, (5, 6, 7)))

    def guarded(condition, act):
        if condition is None:
            act()
        else:
            pl.when(condition)(act)

    barrier = pltpu.get_barrier_semaphore()
    neighbours = jnp.int32(0)
    for n in range(8):
        neighbours = neighbours + inside[n].astype(jnp.int32)

        @pl.when(inside[n])
        def _(n=n):
            pl.semaphore_signal(barrier, inc=1, device_id=ids[n], device_id_type=MESH)

        @pl.when(jnp.logical_not(inside[n]))
        def _(n=n):
            pos_recv[n] = jnp.zeros((4, P_DEV), f32)
            load_recv[n] = jnp.zeros((4, P_DEV), f32)
            req_recv[n] = jnp.zeros((8, 128), f32)
            val_recv[n] = jnp.zeros((8, 128), f32)

    def remote(src, dst, ss, rs, n):
        return pltpu.make_async_remote_copy(
            src_ref=src, dst_ref=dst.at[7 - n], send_sem=ss.at[n], recv_sem=rs.at[7 - n],
            device_id=ids[n], device_id_type=MESH,
        )

    pos_copies = [remote(pos_send, pos_recv, pos_ss, pos_rs, n) for n in range(8)]
    req_copies = [remote(req_send.at[n // 2], req_recv, req_ss, req_rs, n) for n in range(8)]
    val_copies = [remote(val_send.at[n // 2], val_recv, val_ss, val_rs, n) for n in range(8)]
    load_copies = [remote(load_send, load_recv, load_ss, load_rs, n) for n in range(8)]

    loads_in[0].wait()
    fz = frac_ref[2]
    z_own = fz * HEIGHT * DEPTH_SCALE

    def sum_step(i, acc):
        at = (rows_iota((64, P_DEV)) + i * 64).astype(f32)
        d = z_own - (at + 0.5) * (DEPTH_SCALE / BX)
        bumps = jnp.exp2(-(d * d))
        return acc + jnp.sum(bumps.reshape(8, 8, P_DEV), axis=0)

    partial = lax.fori_loop(0, BINS_THIRD_AXIS // 64, sum_step, jnp.zeros((8, P_DEV), f32))
    total = jnp.sum(partial, axis=0, keepdims=True)
    for d in range(3):
        pos_send[d : d + 1, :] = frac_ref[d]
    pos_send[3:4, :] = -LOG2E * jnp.log(total)

    def start_all(copies):
        for n in range(8):
            pl.when(inside[n])(copies[n].start)

    def arrive(copies, m):
        pl.when(inside[m])(copies[7 - m].wait_recv)

    pl.semaphore_wait(barrier, neighbours)
    start_all(pos_copies)

    for copy in loads_in[1:]:
        copy.wait()
    row8 = rows_iota((8, 1))
    offsets = jnp.zeros((8, 1), jnp.int32)
    for n, (dx, dy) in enumerate(STEPS):
        offsets = jnp.where(row8 == n, dx * grid_y + dy, offsets)
    delta = owner_ref[...] - (me_x * grid_y + me_y)
    chosen = jnp.where(delta == offsets, 1.0, 0.0).astype(f32)
    blocks = [chosen[:, 128 * b : 128 * b + 128] for b in range(8)]
    stacked = jnp.concatenate(blocks, axis=0).astype(bf16)
    lower = rows_iota((128, 128)) < lax.broadcasted_iota(jnp.int32, (128, 128), 1)
    earlier = jnp.dot(stacked, jnp.where(lower, 1.0, 0.0).astype(bf16), preferred_element_type=f32)
    base = (row8 * CAP).astype(f32)
    ranked = []
    for b in range(8):
        ranked.append(earlier[8 * b : 8 * b + 8] + base)
        base = base + jnp.sum(blocks[b], axis=1, keepdims=True)
    ranked = jnp.concatenate(ranked, axis=1)
    is_remote = jnp.sum(chosen, axis=0, keepdims=True)
    place = jnp.sum(chosen * ranked, axis=0, keepdims=True)
    slot = jnp.where(is_remote > 0.0, place, -1.0)
    for i in range(8):
        at = (rows_iota((64, 1)) + i * 64).astype(f32)
        g_ref[64 * i : 64 * i + 64, :] = jnp.where(slot == at, 1.0, 0.0).astype(bf16)

    xs[0:1, :] = element_ref[...].astype(f32)
    for d in range(3):
        xs[1 + d : 2 + d, :] = coords_ref[d].astype(f32)
    xs[4:8, :] = jnp.zeros((4, P_DEV), f32)
    payload = xs[...]
    payload16 = jnp.concatenate([payload, jnp.zeros((8, P_DEV), f32)], axis=0).astype(bf16)
    outgoing = lax.dot_general(
        payload16, g_ref[...], (((1,), (1,)), ((), ())), preferred_element_type=f32
    )
    for j in range(4):
        req_send[j] = outgoing[0:8, 128 * j : 128 * j + 128]
    start_all(req_copies)

    def interpolate(requests):
        slots = requests.shape[1]
        levels = rows_iota((QUANT, 1)).astype(f32)
        factors = []
        for axis in range(3):
            select = jnp.where(requests[1 + axis : 2 + axis, :] == levels, 1.0, 0.0).astype(bf16)
            pieces = jnp.dot(basis_ref[...], select, preferred_element_type=f32)
            factors.append(pieces[0:8] + pieces[8:16] + pieces[16:24])
        for a in range(8):
            plane = factors[0][a : a + 1, :] * factors[1]
            for b in range(0, 8, 2):
                pair = jnp.concatenate(
                    [plane[b : b + 1, :] * factors[2], plane[b + 1 : b + 2, :] * factors[2]], axis=0
                )
                at = 64 * a + 8 * b
                weights[at : at + 16, :] = pair.astype(bf16)
        projected = jnp.dot(table_ref[...], weights[...], preferred_element_type=f32)
        mine = requests[0:1, :] == rows_iota((E_DEV, 1)).astype(f32)
        values = [
            jnp.sum(jnp.where(mine, projected[E_DEV * k : E_DEV * k + E_DEV, :], 0.0), axis=0, keepdims=True)
            for k in range(6)
        ]
        values = jnp.concatenate(values + [jnp.zeros((2, slots), f32)], axis=0)
        return values.astype(bf16).astype(f32)

    def place_rows(dx, dy):
        row = rows_iota((8, 1))
        factor = jnp.where(row == 2, HEIGHT * PAIR_SCALE, PAIR_SCALE)
        shift = jnp.where(row == 0, dx * PAIR_SCALE, jnp.where(row == 1, dy * PAIR_SCALE, -0.5 * HEIGHT * PAIR_SCALE))
        return jnp.where(row < 3, xs[...] * factor + shift, 0.0)

    def features(m, dx, dy, weight):
        row = rows_iota((8, 1))
        where_at = place_rows(dx, dy)
        half = 0.5 * jnp.sum(where_at * where_at, axis=0, keepdims=True)
        vector = jnp.where(row == 3, -half, jnp.where(row == 4, 1.0, where_at))
        q1, q2, q3 = split3(vector)
        depth = where_at[2:3, :] * (DEPTH_SCALE / PAIR_SCALE)
        h1, h2, h3 = split3(xs[3:4, :] - depth * depth)
        level = jnp.where(row == 0, h1, jnp.where(row == 1, h2, jnp.where(row == 2, h3, 0.0)))
        stack = jnp.concatenate([q1, q2, q1, q2, q3, q1, level, jnp.zeros_like(level)], axis=0)
        fq_t[m] = stack.T.astype(bf16)
        packed = jnp.where(row < 5, q1, pltpu.roll(q3, 5, axis=0))
        if weight is not None:
            packed, q2 = packed * weight, q2 * weight
        feat[m] = jnp.concatenate([packed, q2], axis=0).astype(bf16)
        return where_at

    xs[0:4, :] = pos_send[...]
    xs[4:8, :] = jnp.zeros((4, P_DEV), f32)
    own_at = features(OWN, 0, 0, None)
    row8 = rows_iota((8, 1))
    half_own = 0.5 * jnp.sum(own_at * own_at, axis=0, keepdims=True)
    p1, p2, p3 = split3(jnp.where(row8 == 3, 1.0, jnp.where(row8 == 4, -half_own, own_at)))
    blank = jnp.zeros_like(p1)
    fp[...] = jnp.concatenate([p1, p1, p2, p2, p1, p3, blank, blank], axis=0).astype(bf16)

    def pair_block(m):
        exponent = jnp.dot(fq_t[m], fp[...], preferred_element_type=f32)
        closeness = jnp.exp2(exponent).astype(bf16)
        return jnp.dot(feat[m], closeness, preferred_element_type=f32)

    def edge_rows(fraction, rows):
        d = fraction - (rows.astype(f32) + (0.5 - MARGIN)) * (1.0 / BX)
        return jnp.exp2((d * d) * (-EDGE_RATE))

    row24 = rows_iota((24, 1))
    order_y = jnp.where(row24 < 16, row24 + 4, jnp.where(row24 < 20, row24 - 16, row24))

    def all_edges(fx, fy):
        bump_x = edge_rows(fx, row24)
        bump_y = edge_rows(fy, order_y)
        scale_x = 1.0 / jnp.sum(bump_x, axis=0, keepdims=True)
        scale_y = 1.0 / jnp.sum(bump_y, axis=0, keepdims=True)
        wx_ref[...] = bump_x * scale_x
        wy_ref[...] = bump_y * scale_y

    def depth_rows(m):
        exponent = jnp.dot(fq_t[m], depth_ref[...], preferred_element_type=f32)
        wz[m] = jnp.exp2(exponent).astype(bf16)

    pair_acc[...] = pair_block(OWN)
    for half in range(2):
        own_val[:, 512 * half : 512 * half + 512] = interpolate(payload[:, 512 * half : 512 * half + 512])
    all_edges(pos_send[0:1, :], pos_send[1:2, :])
    depth_rows(OWN)

    def pair_group(members):
        for m in members:
            arrive(pos_copies, m)
        for m in members:
            xs[0:4, :] = pos_recv[m]
            features(m, STEPS[m][0], STEPS[m][1], present[m])
        pair_acc[...] += sum(pair_block(m) for m in members)

    pair_group(groups[0][1])

    for m in range(8):
        arrive(req_copies, m)
    low_half = lax.broadcasted_iota(jnp.int32, (8, 128), 1) < CAP
    arrived = jnp.concatenate(
        [jnp.where(low_half, req_recv[2 * j + 1], req_recv[2 * j]) for j in range(4)], axis=1
    )
    served = interpolate(arrived)
    for j in range(4):
        val_send[j] = served[:, 128 * j : 128 * j + 128]
    start_all(val_copies)

    for condition, members in groups[1:]:
        guarded(condition, functools.partial(pair_group, members))

    for m in range(8):
        arrive(val_copies, m)
    returned = jnp.concatenate(
        [jnp.where(low_half, val_recv[2 * j], val_recv[2 * j + 1]) for j in range(4)], axis=1
    )
    returned16 = jnp.concatenate([returned, jnp.zeros((8, 512), f32)], axis=0).astype(bf16)
    fetched = jnp.dot(returned16, g_ref[...], preferred_element_type=f32)[0:8]
    fetched = jnp.where(is_remote > 0.0, fetched, own_val[...])
    gradient = pltpu.roll(fetched, 5, axis=0)
    sums = pair_acc[...]
    count = sums[4:5, :]
    sums = sums[0:8] + sums[8:16] + pltpu.roll(sums[0:8], 3, axis=0)
    pair = (STIFFNESS / PAIR_SCALE) * (own_at * count - sums)
    for d in range(3):
        xs[d : d + 1, :] = vel_ref[d]
    volume = vol_ref[...]
    force = drag_ref[...] * (fetched - xs[...]) - volume * gradient + pair
    for d in range(3):
        force_ref[d] = force[d : d + 1]
    force_copy = pltpu.make_async_copy(force_ref, force_out, out_ss.at[0])
    force_copy.start()
    loads = jnp.where(row8 == 3, volume, force)
    load_send[...] = loads[0:4]
    start_all(load_copies)

    def spread_step(a, carry):
        plane = wx_ref[pl.ds(a + MARGIN, 1), :] * wy_ref[0:16, :]
        for c in range(4):
            r0 = pl.multiple_of((c * 16 + a) * 16, 16)
            spread_c[pl.ds(r0, 16), :] = (plane * (load_send[c : c + 1, :] * FIELD_SCALE)).astype(bf16)
        return carry

    lax.fori_loop(0, 16, spread_step, 0)

    for c in range(4):
        part = jnp.dot(spread_c[256 * c : 256 * c + 256, :], wz[OWN], preferred_element_type=f32)
        field_ref[c] = part.reshape(16, 16, BINS_THIRD_AXIS)

    def depth_group(members):
        for m in members:
            depth_rows(m)

    for condition, members in groups:
        guarded(condition, functools.partial(depth_group, members))

    out_copies = [force_copy]

    def write_slabs(first, count, k):
        part = pl.ds(first, count)
        copy = pltpu.make_async_copy(field_ref.at[:, part], field_out.at[:, part], out_ss.at[k])
        copy.start()
        out_copies.append(copy)

    def margin(m):
        dx, dy = STEPS[m]
        arrive(load_copies, m)
        all_edges(pos_recv[m, 0:1, :], pos_recv[m, 1:2, :])
        loads_m = [load_recv[m, c : c + 1, :] * FIELD_SCALE for c in range(4)]
        source_x = {-1: 20, 0: 4, 1: 0}[dx]
        target_x = {-1: 0, 0: 0, 1: 12}[dx]
        count_x = 16 if dx == 0 else 4
        if dy == 0:
            for a in range(count_x):
                plane = wx_ref[source_x + a : source_x + a + 1, :] * wy_ref[0:16, :]
                for c in range(4):
                    r0 = (c * count_x + a) * 16
                    spread_e[r0 : r0 + 16, :] = (plane * loads_m[c]).astype(bf16)
            part = jnp.dot(spread_e[...], wz[m], preferred_element_type=f32)
            for c in range(4):
                field_ref[c, target_x : target_x + 4] += part[64 * c : 64 * c + 64].reshape(4, 16, BINS_THIRD_AXIS)
        else:
            first = 20 if dy == -1 else 16
            target_y = 0 if dy == -1 else 12
            wy4[0:4, :] = wy_ref[first : first + 4, :]
            wy4[4:8, :] = wy_ref[first : first + 4, :]
            top = rows_iota((8, 1)) < 4
            for a in range(0, count_x, 4):
                planes = []
                for pair_at in (a, a + 2):
                    s = source_x + pair_at
                    planes.append(jnp.where(top, wx_ref[s : s + 1, :], wx_ref[s + 1 : s + 2, :]) * wy4[...])
                plane = jnp.concatenate(planes, axis=0)
                for c in range(4):
                    r0 = (c * count_x + a) * 4
                    spread_e[r0 : r0 + 16, :] = (plane * loads_m[c]).astype(bf16)
            used = 16 * count_x
            part = jnp.dot(spread_e[0:used, :], wz[m], preferred_element_type=f32)
            for c in range(4):
                for a in range(count_x):
                    r0 = (c * count_x + a) * 4
                    field_ref[c, target_x + a, target_y : target_y + 4, :] += part[r0 : r0 + 4, :]


    def margin_group(members):
        for m in members:
            margin(m)

    for k, (first, count_x) in enumerate(((4, 8), (0, 4), (12, 4))):
        condition, members = groups[k]
        guarded(condition, functools.partial(margin_group, members))
        write_slabs(first, count_x, 1 + k)
    for copy in out_copies:
        copy.wait()
    for copies in (pos_copies, req_copies, val_copies, load_copies):
        for n in range(8):
            pl.when(inside[n])(copies[n].wait_send)


def publish(force_in, field_in, force_out, field_out, force_v, field_v, in_sems, out_sems):
    pairs = [(force_in, force_v, force_out)]
    for c in range(4):
        for k in range(4):
            part = pl.ds(4 * k, 4)
            pairs.append((field_in.at[c, part], field_v.at[c, part], field_out.at[c, part]))
    ins = [pltpu.make_async_copy(a, v, in_sems.at[i]) for i, (a, v, o) in enumerate(pairs)]
    outs = [pltpu.make_async_copy(v, o, out_sems.at[i]) for i, (a, v, o) in enumerate(pairs)]
    for copy in ins:
        copy.start()
    for first, second in zip(ins, outs):
        first.wait()
        second.start()
    for copy in outs:
        copy.wait()


def body(fractions, velocity, drag_rate, volume, owner, element, coords, fluid):
    grid_x = lax.axis_size("gx")
    grid_y = lax.axis_size("gy")
    table = jnp.transpose(fluid.reshape(E_DEV, 6, 512), (1, 0, 2)).reshape(E_DEV * 6, 512)
    hbm = pl.BlockSpec(memory_space=pl.ANY)
    dma = pltpu.SemaphoreType.DMA((8,))
    force, field = pl.pallas_call(
        functools.partial(kernel, grid_x, grid_y),
        out_shape=(
            jax.ShapeDtypeStruct((3, 1, P_DEV), f32),
            jax.ShapeDtypeStruct((4, BX, BY, BINS_THIRD_AXIS), f32),
        ),
        in_specs=[hbm] * 10,
        out_specs=(hbm, hbm),
        scratch_shapes=[
            pltpu.VMEM((3, 1, P_DEV), f32),
            pltpu.VMEM((4, BX, BY, BINS_THIRD_AXIS), f32),
            pltpu.VMEM((3, 1, P_DEV), f32),
            pltpu.VMEM((3, 1, P_DEV), f32),
            pltpu.VMEM((1, P_DEV), f32),
            pltpu.VMEM((1, P_DEV), f32),
            pltpu.VMEM((1, P_DEV), jnp.int32),
            pltpu.VMEM((1, P_DEV), jnp.int32),
            pltpu.VMEM((3, 1, P_DEV), jnp.int32),
            pltpu.VMEM((6 * E_DEV, 512), bf16),
            pltpu.VMEM((32, QUANT), bf16),
            pltpu.VMEM((ROWS_Q, BINS_THIRD_AXIS), bf16),
            pltpu.VMEM((4, P_DEV), f32),
            pltpu.VMEM((8, 4, P_DEV), f32),
            pltpu.VMEM((4, 8, 128), f32),
            pltpu.VMEM((8, 8, 128), f32),
            pltpu.VMEM((4, 8, 128), f32),
            pltpu.VMEM((8, 8, 128), f32),
            pltpu.VMEM((4, P_DEV), f32),
            pltpu.VMEM((8, 4, P_DEV), f32),
            pltpu.VMEM((8, P_DEV), f32),
            pltpu.VMEM((9, P_DEV, ROWS_Q), bf16),
            pltpu.VMEM((9, 16, P_DEV), bf16),
            pltpu.VMEM((ROWS_Q, P_DEV), bf16),
            pltpu.VMEM((8 * CAP, P_DEV), bf16),
            pltpu.VMEM((512, 512), bf16),
            pltpu.VMEM((8, P_DEV), f32),
            pltpu.VMEM((16, P_DEV), f32),
            pltpu.VMEM((9, P_DEV, BINS_THIRD_AXIS), bf16),
            pltpu.VMEM((1024, P_DEV), bf16),
            pltpu.VMEM((256, P_DEV), bf16),
            pltpu.VMEM((24, P_DEV), f32),
            pltpu.VMEM((24, P_DEV), f32),
            pltpu.VMEM((24, P_DEV), f32),
            pltpu.VMEM((8, P_DEV), f32),
        ]
        + [pltpu.SemaphoreType.DMA((10,)), pltpu.SemaphoreType.DMA((4,))] + [dma] * 8,
        compiler_params=pltpu.CompilerParams(
            collective_id=0, has_side_effects=True, vmem_limit_bytes=60 * 1024 * 1024
        ),
        name="particle_step",
    )(
        fractions.reshape(3, 1, P_DEV),
        velocity.reshape(3, 1, P_DEV),
        drag_rate.reshape(1, P_DEV),
        volume.reshape(1, P_DEV),
        owner.reshape(1, P_DEV),
        element.reshape(1, P_DEV),
        coords.reshape(3, 1, P_DEV),
        table,
        jnp.asarray(basis_pieces()),
        jnp.asarray(depth_pieces()),
    )
    force, field = pl.pallas_call(
        publish,
        out_shape=(
            jax.ShapeDtypeStruct((3, 1, P_DEV), f32),
            jax.ShapeDtypeStruct((4, BX, BY, BINS_THIRD_AXIS), f32),
        ),
        in_specs=[hbm] * 2,
        out_specs=(hbm, hbm),
        scratch_shapes=[
            pltpu.VMEM((3, 1, P_DEV), f32),
            pltpu.VMEM((4, BX, BY, BINS_THIRD_AXIS), f32),
            pltpu.SemaphoreType.DMA((17,)),
            pltpu.SemaphoreType.DMA((17,)),
        ],
        compiler_params=pltpu.CompilerParams(vmem_limit_bytes=60 * 1024 * 1024),
        name="publish",
    )(force, field)
    return force.reshape(1, 1, 3, P_DEV), field


def solution(mesh):
    return jax.shard_map(
        body,
        mesh=mesh,
        in_specs=(
            P("gx", "gy", None, None),
            P("gx", "gy", None, None),
            P("gx", "gy", None),
            P("gx", "gy", None),
            P("gx", "gy", None, None),
            P("gx", "gy", None),
            P("gx", "gy", None, None),
            P("gx", "gy", None, None, None),
        ),
        out_specs=(P("gx", "gy", None, None), P(None, "gx", "gy", None)),
        check_vma=False,
    )
```

```python
import functools
import math

import jax
import jax.numpy as jnp
import numpy as np
from jax import lax
from jax.experimental import pallas as pl
from jax.experimental.pallas import tpu as pltpu
from jax.sharding import PartitionSpec as P

P_DEV = 1024
E_DEV = 32
BINS_THIRD_AXIS = 512
BX = 16
BY = 16
MARGIN = 4
QUANT = 64
CAP = 64

GLL_NODES = (
    -1.0,
    -0.8717401485096066,
    -0.5917001814331423,
    -0.2092992179024789,
    0.2092992179024789,
    0.5917001814331423,
    0.8717401485096066,
    1.0,
)
STIFFNESS = 0.5
PAIR_WIDTH = 0.3
FILTER_BINS = 3.0

f32 = jnp.float32
bf16 = jnp.bfloat16
MESH = pl.DeviceIdType.MESH

LOG2E = math.log2(math.e)
HEIGHT = BINS_THIRD_AXIS / BX
PAIR_SCALE = math.sqrt(LOG2E) / PAIR_WIDTH
DEPTH_SCALE = math.sqrt(LOG2E / 2.0) / (FILTER_BINS / BX)
EDGE_RATE = LOG2E / (2.0 * (FILTER_BINS / BX) ** 2)
FIELD_SCALE = BX * BY * BINS_THIRD_AXIS / P_DEV

STEPS = tuple((k // 3 - 1, k % 3 - 1) for k in range(9) if k != 4)
OWN = 8
ROWS_Q = 64


def basis_pieces():
    points = -1.0 + (2.0 * np.arange(QUANT) + 1.0) / QUANT
    lagrange = np.ones((QUANT, 8))
    for node_a in range(8):
        for node_b in range(8):
            if node_b != node_a:
                lagrange[:, node_a] *= (points - GLL_NODES[node_b]) / (
                    GLL_NODES[node_a] - GLL_NODES[node_b]
                )
    rest = lagrange.astype(np.float32).T
    pieces = []
    for _ in range(3):
        piece = rest.astype(bf16)
        pieces.append(piece)
        rest = rest - piece.astype(np.float32)
    pieces.append(np.zeros_like(pieces[0]))
    return np.concatenate(pieces, axis=0)


def depth_pieces():
    centres = ((np.arange(BINS_THIRD_AXIS) + 0.5) / BX - 0.5 * HEIGHT) * DEPTH_SCALE
    rows = np.zeros((8, BINS_THIRD_AXIS))
    rows[2] = 2.0 * centres * (DEPTH_SCALE / PAIR_SCALE)
    rows[4] = -centres * centres
    pieces = []
    for _ in range(3):
        piece = rows.astype(bf16)
        pieces.append(piece)
        rows = rows - piece.astype(np.float64)
    first, second, third = pieces
    last = np.zeros((16, BINS_THIRD_AXIS))
    last[0:3] = 1.0
    return np.concatenate([first, first, second, second, first, third, last.astype(bf16)], axis=0)


def rows_iota(shape):
    return lax.broadcasted_iota(jnp.int32, shape, 0)


def split3(x):
    high = x.astype(bf16).astype(f32)
    rest = x - high
    middle = rest.astype(bf16).astype(f32)
    low = (rest - middle).astype(bf16).astype(f32)
    return high, middle, low


def kernel(
    grid_x, grid_y,
    frac_in, vel_in, drag_in, vol_in, owner_in, element_in, coords_in, table_in, basis_in, depth_in,
    force_out, field_out,
    force_ref, field_ref,
    frac_ref, vel_ref, drag_ref, vol_ref, owner_ref, element_ref, coords_ref, table_ref, basis_ref, depth_ref,
    pos_send, pos_recv, req_send, req_recv, val_send, val_recv, load_send, load_recv,
    xs, close, fq_t, feat, fp, g_ref, weights, own_val, pair_acc, wz, spread_c, spread_e, wx_ref, wy_ref,
    wy4,
    in_ss, out_ss, pos_ss, pos_rs, req_ss, req_rs, val_ss, val_rs, load_ss, load_rs,
):
    inputs = (
        (frac_in, frac_ref), (owner_in, owner_ref), (element_in, element_ref), (coords_in, coords_ref),
        (basis_in, basis_ref), (table_in, table_ref), (vel_in, vel_ref), (drag_in, drag_ref), (vol_in, vol_ref),
        (depth_in, depth_ref),
    )
    loads_in = [pltpu.make_async_copy(src, dst, in_ss.at[k]) for k, (src, dst) in enumerate(inputs)]
    for copy in loads_in:
        copy.start()

    me_x = lax.axis_index("gx")
    me_y = lax.axis_index("gy")
    ids = []
    present = []
    inside = []
    for dx, dy in STEPS:
        tx, ty = me_x + dx, me_y + dy
        ids.append((lax.rem(tx + grid_x, grid_x), lax.rem(ty + grid_y, grid_y)))
        within = (tx >= 0) & (tx < grid_x) & (ty >= 0) & (ty < grid_y)
        inside.append(within)
        present.append(jnp.where(within, 1.0, 0.0).astype(f32))
    groups = ((None, (3, 4)), (me_x > 0, (0, 1, 2)), (me_x < grid_x - 1, (5, 6, 7)))

    def guarded(condition, act):
        if condition is None:
            act()
        else:
            pl.when(condition)(act)

    barrier = pltpu.get_barrier_semaphore()
    neighbours = jnp.int32(0)
    for n in range(8):
        neighbours = neighbours + inside[n].astype(jnp.int32)

        @pl.when(inside[n])
        def _(n=n):
            pl.semaphore_signal(barrier, inc=1, device_id=ids[n], device_id_type=MESH)

        @pl.when(jnp.logical_not(inside[n]))
        def _(n=n):
            pos_recv[n] = jnp.zeros((4, P_DEV), f32)
            load_recv[n] = jnp.zeros((4, P_DEV), f32)
            req_recv[n] = jnp.zeros((8, 128), f32)
            val_recv[n] = jnp.zeros((8, 128), f32)

    def remote(src, dst, ss, rs, n):
        return pltpu.make_async_remote_copy(
            src_ref=src, dst_ref=dst.at[7 - n], send_sem=ss.at[n], recv_sem=rs.at[7 - n],
            device_id=ids[n], device_id_type=MESH,
        )

    pos_copies = [remote(pos_send, pos_recv, pos_ss, pos_rs, n) for n in range(8)]
    req_copies = [remote(req_send.at[n // 2], req_recv, req_ss, req_rs, n) for n in range(8)]
    val_copies = [remote(val_send.at[n // 2], val_recv, val_ss, val_rs, n) for n in range(8)]
    load_copies = [remote(load_send, load_recv, load_ss, load_rs, n) for n in range(8)]

    loads_in[0].wait()
    fz = frac_ref[2]
    z_own = fz * HEIGHT * DEPTH_SCALE

    def sum_step(i, acc):
        at = (rows_iota((64, P_DEV)) + i * 64).astype(f32)
        d = z_own - (at + 0.5) * (DEPTH_SCALE / BX)
        bumps = jnp.exp2(-(d * d))
        return acc + jnp.sum(bumps.reshape(8, 8, P_DEV), axis=0)

    partial = lax.fori_loop(0, BINS_THIRD_AXIS // 64, sum_step, jnp.zeros((8, P_DEV), f32))
    total = jnp.sum(partial, axis=0, keepdims=True)
    for d in range(3):
        pos_send[d : d + 1, :] = frac_ref[d]
    pos_send[3:4, :] = -LOG2E * jnp.log(total)

    def start_all(copies):
        for n in range(8):
            pl.when(inside[n])(copies[n].start)

    def arrive(copies, m):
        pl.when(inside[m])(copies[7 - m].wait_recv)

    pl.semaphore_wait(barrier, neighbours)
    start_all(pos_copies)

    for copy in loads_in[1:]:
        copy.wait()
    row8 = rows_iota((8, 1))
    offsets = jnp.zeros((8, 1), jnp.int32)
    for n, (dx, dy) in enumerate(STEPS):
        offsets = jnp.where(row8 == n, dx * grid_y + dy, offsets)
    delta = owner_ref[...] - (me_x * grid_y + me_y)
    chosen = jnp.where(delta == offsets, 1.0, 0.0).astype(f32)
    blocks = [chosen[:, 128 * b : 128 * b + 128] for b in range(8)]
    stacked = jnp.concatenate(blocks, axis=0).astype(bf16)
    lower = rows_iota((128, 128)) < lax.broadcasted_iota(jnp.int32, (128, 128), 1)
    earlier = jnp.dot(stacked, jnp.where(lower, 1.0, 0.0).astype(bf16), preferred_element_type=f32)
    base = (row8 * CAP).astype(f32)
    ranked = []
    for b in range(8):
        ranked.append(earlier[8 * b : 8 * b + 8] + base)
        base = base + jnp.sum(blocks[b], axis=1, keepdims=True)
    ranked = jnp.concatenate(ranked, axis=1)
    is_remote = jnp.sum(chosen, axis=0, keepdims=True)
    place = jnp.sum(chosen * ranked, axis=0, keepdims=True)
    slot = jnp.where(is_remote > 0.0, place, -1.0)
    for i in range(8):
        at = (rows_iota((64, 1)) + i * 64).astype(f32)
        g_ref[64 * i : 64 * i + 64, :] = jnp.where(slot == at, 1.0, 0.0).astype(bf16)

    xs[0:1, :] = element_ref[...].astype(f32)
    for d in range(3):
        xs[1 + d : 2 + d, :] = coords_ref[d].astype(f32)
    xs[4:8, :] = jnp.zeros((4, P_DEV), f32)
    payload = xs[...]
    payload16 = jnp.concatenate([payload, jnp.zeros((8, P_DEV), f32)], axis=0).astype(bf16)
    outgoing = lax.dot_general(
        payload16, g_ref[...], (((1,), (1,)), ((), ())), preferred_element_type=f32
    )
    for j in range(4):
        req_send[j] = outgoing[0:8, 128 * j : 128 * j + 128]
    start_all(req_copies)

    def interpolate(requests):
        slots = requests.shape[1]
        levels = rows_iota((QUANT, 1)).astype(f32)
        factors = []
        for axis in range(3):
            select = jnp.where(requests[1 + axis : 2 + axis, :] == levels, 1.0, 0.0).astype(bf16)
            pieces = jnp.dot(basis_ref[...], select, preferred_element_type=f32)
            factors.append(pieces[0:8] + pieces[8:16] + pieces[16:24])
        for a in range(8):
            plane = factors[0][a : a + 1, :] * factors[1]
            for b in range(0, 8, 2):
                pair = jnp.concatenate(
                    [plane[b : b + 1, :] * factors[2], plane[b + 1 : b + 2, :] * factors[2]], axis=0
                )
                at = 64 * a + 8 * b
                weights[at : at + 16, :] = pair.astype(bf16)
        projected = jnp.dot(table_ref[...], weights[...], preferred_element_type=f32)
        mine = requests[0:1, :] == rows_iota((E_DEV, 1)).astype(f32)
        values = [
            jnp.sum(jnp.where(mine, projected[E_DEV * k : E_DEV * k + E_DEV, :], 0.0), axis=0, keepdims=True)
            for k in range(6)
        ]
        values = jnp.concatenate(values + [jnp.zeros((2, slots), f32)], axis=0)
        return values.astype(bf16).astype(f32)

    def place_rows(dx, dy):
        row = rows_iota((8, 1))
        factor = jnp.where(row == 2, HEIGHT * PAIR_SCALE, PAIR_SCALE)
        shift = jnp.where(row == 0, dx * PAIR_SCALE, jnp.where(row == 1, dy * PAIR_SCALE, -0.5 * HEIGHT * PAIR_SCALE))
        return jnp.where(row < 3, xs[...] * factor + shift, 0.0)

    def features(m, dx, dy, weight):
        row = rows_iota((8, 1))
        where_at = place_rows(dx, dy)
        half = 0.5 * jnp.sum(where_at * where_at, axis=0, keepdims=True)
        vector = jnp.where(row == 3, -half, jnp.where(row == 4, 1.0, where_at))
        q1, q2, q3 = split3(vector)
        depth = where_at[2:3, :] * (DEPTH_SCALE / PAIR_SCALE)
        h1, h2, h3 = split3(xs[3:4, :] - depth * depth)
        level = jnp.where(row == 0, h1, jnp.where(row == 1, h2, jnp.where(row == 2, h3, 0.0)))
        stack = jnp.concatenate([q1, q2, q1, q2, q3, q1, level, jnp.zeros_like(level)], axis=0)
        fq_t[m] = stack.T.astype(bf16)
        packed = jnp.where(row < 5, q1, pltpu.roll(q3, 5, axis=0))
        if weight is not None:
            packed, q2 = packed * weight, q2 * weight
        feat[m] = jnp.concatenate([packed, q2], axis=0).astype(bf16)
        return where_at

    xs[0:4, :] = pos_send[...]
    xs[4:8, :] = jnp.zeros((4, P_DEV), f32)
    own_at = features(OWN, 0, 0, None)
    row8 = rows_iota((8, 1))
    half_own = 0.5 * jnp.sum(own_at * own_at, axis=0, keepdims=True)
    p1, p2, p3 = split3(jnp.where(row8 == 3, 1.0, jnp.where(row8 == 4, -half_own, own_at)))
    blank = jnp.zeros_like(p1)
    fp[...] = jnp.concatenate([p1, p1, p2, p2, p1, p3, blank, blank], axis=0).astype(bf16)

    def exponentials(m, turn):
        exponent = jnp.dot(fq_t[m], fp[...], preferred_element_type=f32)
        close[turn] = jnp.exp2(exponent).astype(bf16)

    def pair_sums(m, turn):
        return jnp.dot(feat[m], close[turn], preferred_element_type=f32)

    def edge_rows(fraction, rows):
        d = fraction - (rows.astype(f32) + (0.5 - MARGIN)) * (1.0 / BX)
        return jnp.exp2((d * d) * (-EDGE_RATE))

    row24 = rows_iota((24, 1))
    order_y = jnp.where(row24 < 16, row24 + 4, jnp.where(row24 < 20, row24 - 16, row24))

    def all_edges(m, fx, fy):
        bump_x = edge_rows(fx, row24)
        bump_y = edge_rows(fy, order_y)
        scale_x = 1.0 / jnp.sum(bump_x, axis=0, keepdims=True)
        scale_y = 1.0 / jnp.sum(bump_y, axis=0, keepdims=True)
        wx_ref[m] = bump_x * scale_x
        wy_ref[m] = bump_y * scale_y

    def depth_rows(m):
        exponent = jnp.dot(fq_t[m], depth_ref[...], preferred_element_type=f32)
        wz[m] = jnp.exp2(exponent).astype(bf16)

    exponentials(OWN, 0)
    for half in range(2):
        own_val[:, 512 * half : 512 * half + 512] = interpolate(payload[:, 512 * half : 512 * half + 512])
    all_edges(OWN, pos_send[0:1, :], pos_send[1:2, :])
    depth_rows(OWN)

    def pair_group(members, turns, before, turn_before, first):
        for m in members:
            arrive(pos_copies, m)
        for m in members:
            xs[0:4, :] = pos_recv[m]
            features(m, STEPS[m][0], STEPS[m][1], present[m])
        acc = None if first else pair_acc[...]
        for m, turn in zip(members, turns):
            term = pair_sums(before, turn_before)
            exponentials(m, turn)
            acc = term if acc is None else acc + term
            before, turn_before = m, turn
        pair_acc[...] = acc

    pair_group((3, 4), (1, 0), OWN, 0, True)

    for m in range(8):
        arrive(req_copies, m)
    low_half = lax.broadcasted_iota(jnp.int32, (8, 128), 1) < CAP
    arrived = jnp.concatenate(
        [jnp.where(low_half, req_recv[2 * j + 1], req_recv[2 * j]) for j in range(4)], axis=1
    )
    served = interpolate(arrived)
    for j in range(4):
        val_send[j] = served[:, 128 * j : 128 * j + 128]
    start_all(val_copies)

    has_lower, has_upper = groups[1][0], groups[2][0]
    guarded(has_lower, lambda: pair_group((0, 1, 2), (1, 0, 1), 4, 0, False))
    block_before = jnp.where(has_lower, 2, 4)
    turn_before = jnp.where(has_lower, 1, 0)
    guarded(has_upper, lambda: pair_group((5, 6, 7), (2, 0, 1), block_before, turn_before, False))
    pair_acc[...] += pair_sums(jnp.where(has_upper, 7, 2), 1)

    for m in range(8):
        arrive(val_copies, m)
    returned = jnp.concatenate(
        [jnp.where(low_half, val_recv[2 * j], val_recv[2 * j + 1]) for j in range(4)], axis=1
    )
    returned16 = jnp.concatenate([returned, jnp.zeros((8, 512), f32)], axis=0).astype(bf16)
    fetched = jnp.dot(returned16, g_ref[...], preferred_element_type=f32)[0:8]
    fetched = jnp.where(is_remote > 0.0, fetched, own_val[...])
    gradient = pltpu.roll(fetched, 5, axis=0)
    sums = pair_acc[...]
    count = sums[4:5, :]
    sums = sums[0:8] + sums[8:16] + pltpu.roll(sums[0:8], 3, axis=0)
    pair = (STIFFNESS / PAIR_SCALE) * (own_at * count - sums)
    for d in range(3):
        xs[d : d + 1, :] = vel_ref[d]
    volume = vol_ref[...]
    force = drag_ref[...] * (fetched - xs[...]) - volume * gradient + pair
    for d in range(3):
        force_ref[d] = force[d : d + 1]
    force_copy = pltpu.make_async_copy(force_ref, force_out, out_ss.at[0])
    force_copy.start()
    loads = jnp.where(row8 == 3, volume, force)
    load_send[...] = loads[0:4]
    start_all(load_copies)

    def spread_step(a, carry):
        plane = wx_ref[OWN, pl.ds(a + MARGIN, 1), :] * wy_ref[OWN, 0:16, :]
        for c in range(4):
            r0 = pl.multiple_of((c * 16 + a) * 16, 16)
            spread_c[pl.ds(r0, 16), :] = (plane * (load_send[c : c + 1, :] * FIELD_SCALE)).astype(bf16)
        return carry

    lax.fori_loop(0, 16, spread_step, 0)

    for c in range(4):
        part = jnp.dot(spread_c[256 * c : 256 * c + 256, :], wz[OWN], preferred_element_type=f32)
        field_ref[c] = part.reshape(16, 16, BINS_THIRD_AXIS)

    def depth_group(members):
        for m in members:
            all_edges(m, pos_recv[m, 0:1, :], pos_recv[m, 1:2, :])
            depth_rows(m)

    for condition, members in groups:
        guarded(condition, functools.partial(depth_group, members))

    out_copies = [force_copy]

    def write_slabs(first, count, k):
        part = pl.ds(first, count)
        copy = pltpu.make_async_copy(field_ref.at[:, part], field_out.at[:, part], out_ss.at[k])
        copy.start()
        out_copies.append(copy)

    def spread_margin(m, k):
        dx, dy = STEPS[m]
        loads_m = [load_recv[m, c : c + 1, :] * FIELD_SCALE for c in range(4)]
        source_x = {-1: 20, 0: 4, 1: 0}[dx]
        count_x = 16 if dx == 0 else 4
        if dy == 0:
            for a in range(count_x):
                plane = wx_ref[m, source_x + a : source_x + a + 1, :] * wy_ref[m, 0:16, :]
                for c in range(4):
                    r0 = (c * count_x + a) * 16
                    spread_e[k, r0 : r0 + 16, :] = (plane * loads_m[c]).astype(bf16)
        else:
            first = 20 if dy == -1 else 16
            wy4[k, 0:4, :] = wy_ref[m, first : first + 4, :]
            wy4[k, 4:8, :] = wy_ref[m, first : first + 4, :]
            top = rows_iota((8, 1)) < 4
            for a in range(0, count_x, 4):
                planes = []
                for pair_at in (a, a + 2):
                    s = source_x + pair_at
                    planes.append(
                        jnp.where(top, wx_ref[m, s : s + 1, :], wx_ref[m, s + 1 : s + 2, :]) * wy4[k]
                    )
                plane = jnp.concatenate(planes, axis=0)
                for c in range(4):
                    r0 = (c * count_x + a) * 4
                    spread_e[k, r0 : r0 + 16, :] = (plane * loads_m[c]).astype(bf16)

    def add_margin(m, k):
        dx, dy = STEPS[m]
        target_x = {-1: 0, 0: 0, 1: 12}[dx]
        count_x = 16 if dx == 0 else 4
        used = 256 if dy == 0 else 16 * count_x
        part = jnp.dot(spread_e[k, 0:used, :], wz[m], preferred_element_type=f32)
        if dy == 0:
            for c in range(4):
                field_ref[c, target_x : target_x + 4] += part[64 * c : 64 * c + 64].reshape(4, 16, BINS_THIRD_AXIS)
        else:
            target_y = 0 if dy == -1 else 12
            for c in range(4):
                for a in range(count_x):
                    r0 = (c * count_x + a) * 4
                    field_ref[c, target_x + a, target_y : target_y + 4, :] += part[r0 : r0 + 4, :]

    def margin_group(members):
        for m in members:
            arrive(load_copies, m)
        for k, m in enumerate(members):
            spread_margin(m, k)
        for k, m in enumerate(members):
            add_margin(m, k)

    for k, (first, count_x) in enumerate(((4, 8), (0, 4), (12, 4))):
        condition, members = groups[k]
        guarded(condition, functools.partial(margin_group, members))
        write_slabs(first, count_x, 1 + k)
    for copy in out_copies:
        copy.wait()
    for copies in (pos_copies, req_copies, val_copies, load_copies):
        for n in range(8):
            pl.when(inside[n])(copies[n].wait_send)


def publish(force_in, field_in, force_out, field_out, force_v, field_v, in_sems, out_sems):
    pairs = [(force_in, force_v, force_out)]
    for c in range(4):
        for k in range(4):
            part = pl.ds(4 * k, 4)
            pairs.append((field_in.at[c, part], field_v.at[c, part], field_out.at[c, part]))
    ins = [pltpu.make_async_copy(a, v, in_sems.at[i]) for i, (a, v, o) in enumerate(pairs)]
    outs = [pltpu.make_async_copy(v, o, out_sems.at[i]) for i, (a, v, o) in enumerate(pairs)]
    for copy in ins:
        copy.start()
    for first, second in zip(ins, outs):
        first.wait()
        second.start()
    for copy in outs:
        copy.wait()


def body(fractions, velocity, drag_rate, volume, owner, element, coords, fluid):
    grid_x = lax.axis_size("gx")
    grid_y = lax.axis_size("gy")
    table = jnp.transpose(fluid.reshape(E_DEV, 6, 512), (1, 0, 2)).reshape(E_DEV * 6, 512)
    hbm = pl.BlockSpec(memory_space=pl.ANY)
    dma = pltpu.SemaphoreType.DMA((8,))
    force, field = pl.pallas_call(
        functools.partial(kernel, grid_x, grid_y),
        out_shape=(
            jax.ShapeDtypeStruct((3, 1, P_DEV), f32),
            jax.ShapeDtypeStruct((4, BX, BY, BINS_THIRD_AXIS), f32),
        ),
        in_specs=[hbm] * 10,
        out_specs=(hbm, hbm),
        scratch_shapes=[
            pltpu.VMEM((3, 1, P_DEV), f32),
            pltpu.VMEM((4, BX, BY, BINS_THIRD_AXIS), f32),
            pltpu.VMEM((3, 1, P_DEV), f32),
            pltpu.VMEM((3, 1, P_DEV), f32),
            pltpu.VMEM((1, P_DEV), f32),
            pltpu.VMEM((1, P_DEV), f32),
            pltpu.VMEM((1, P_DEV), jnp.int32),
            pltpu.VMEM((1, P_DEV), jnp.int32),
            pltpu.VMEM((3, 1, P_DEV), jnp.int32),
            pltpu.VMEM((6 * E_DEV, 512), bf16),
            pltpu.VMEM((32, QUANT), bf16),
            pltpu.VMEM((ROWS_Q, BINS_THIRD_AXIS), bf16),
            pltpu.VMEM((4, P_DEV), f32),
            pltpu.VMEM((8, 4, P_DEV), f32),
            pltpu.VMEM((4, 8, 128), f32),
            pltpu.VMEM((8, 8, 128), f32),
            pltpu.VMEM((4, 8, 128), f32),
            pltpu.VMEM((8, 8, 128), f32),
            pltpu.VMEM((4, P_DEV), f32),
            pltpu.VMEM((8, 4, P_DEV), f32),
            pltpu.VMEM((8, P_DEV), f32),
            pltpu.VMEM((3, P_DEV, P_DEV), bf16),
            pltpu.VMEM((9, P_DEV, ROWS_Q), bf16),
            pltpu.VMEM((9, 16, P_DEV), bf16),
            pltpu.VMEM((ROWS_Q, P_DEV), bf16),
            pltpu.VMEM((8 * CAP, P_DEV), bf16),
            pltpu.VMEM((512, 512), bf16),
            pltpu.VMEM((8, P_DEV), f32),
            pltpu.VMEM((16, P_DEV), f32),
            pltpu.VMEM((9, P_DEV, BINS_THIRD_AXIS), bf16),
            pltpu.VMEM((1024, P_DEV), bf16),
            pltpu.VMEM((3, 256, P_DEV), bf16),
            pltpu.VMEM((9, 24, P_DEV), f32),
            pltpu.VMEM((9, 24, P_DEV), f32),
            pltpu.VMEM((3, 8, P_DEV), f32),
        ]
        + [pltpu.SemaphoreType.DMA((10,)), pltpu.SemaphoreType.DMA((4,))] + [dma] * 8,
        compiler_params=pltpu.CompilerParams(
            collective_id=0, has_side_effects=True, vmem_limit_bytes=60 * 1024 * 1024
        ),
        name="particle_step",
    )(
        fractions.reshape(3, 1, P_DEV),
        velocity.reshape(3, 1, P_DEV),
        drag_rate.reshape(1, P_DEV),
        volume.reshape(1, P_DEV),
        owner.reshape(1, P_DEV),
        element.reshape(1, P_DEV),
        coords.reshape(3, 1, P_DEV),
        table,
        jnp.asarray(basis_pieces()),
        jnp.asarray(depth_pieces()),
    )
    force, field = pl.pallas_call(
        publish,
        out_shape=(
            jax.ShapeDtypeStruct((3, 1, P_DEV), f32),
            jax.ShapeDtypeStruct((4, BX, BY, BINS_THIRD_AXIS), f32),
        ),
        in_specs=[hbm] * 2,
        out_specs=(hbm, hbm),
        scratch_shapes=[
            pltpu.VMEM((3, 1, P_DEV), f32),
            pltpu.VMEM((4, BX, BY, BINS_THIRD_AXIS), f32),
            pltpu.SemaphoreType.DMA((17,)),
            pltpu.SemaphoreType.DMA((17,)),
        ],
        compiler_params=pltpu.CompilerParams(vmem_limit_bytes=60 * 1024 * 1024),
        name="publish",
    )(force, field)
    return force.reshape(1, 1, 3, P_DEV), field


def solution(mesh):
    return jax.shard_map(
        body,
        mesh=mesh,
        in_specs=(
            P("gx", "gy", None, None),
            P("gx", "gy", None, None),
            P("gx", "gy", None),
            P("gx", "gy", None),
            P("gx", "gy", None, None),
            P("gx", "gy", None),
            P("gx", "gy", None, None),
            P("gx", "gy", None, None, None),
        ),
        out_specs=(P("gx", "gy", None, None), P(None, "gx", "gy", None)),
        check_vma=False,
    )
```

```python
import functools
import math

import jax
import jax.numpy as jnp
import numpy as np
from jax import lax
from jax.experimental import pallas as pl
from jax.experimental.pallas import tpu as pltpu
from jax.sharding import PartitionSpec as P

P_DEV = 1024
E_DEV = 32
BINS_THIRD_AXIS = 512
BX = 16
BY = 16
MARGIN = 4
QUANT = 64
CAP = 64

GLL_NODES = (
    -1.0,
    -0.8717401485096066,
    -0.5917001814331423,
    -0.2092992179024789,
    0.2092992179024789,
    0.5917001814331423,
    0.8717401485096066,
    1.0,
)
STIFFNESS = 0.5
PAIR_WIDTH = 0.3
FILTER_BINS = 3.0

f32 = jnp.float32
bf16 = jnp.bfloat16
MESH = pl.DeviceIdType.MESH

LOG2E = math.log2(math.e)
HEIGHT = BINS_THIRD_AXIS / BX
PAIR_SCALE = math.sqrt(LOG2E) / PAIR_WIDTH
DEPTH_SCALE = math.sqrt(LOG2E / 2.0) / (FILTER_BINS / BX)
EDGE_RATE = LOG2E / (2.0 * (FILTER_BINS / BX) ** 2)
FIELD_SCALE = BX * BY * BINS_THIRD_AXIS / P_DEV

STEPS = tuple((k // 3 - 1, k % 3 - 1) for k in range(9) if k != 4)
OWN = 8
ROWS_Q = 64


def basis_pieces():
    points = -1.0 + (2.0 * np.arange(QUANT) + 1.0) / QUANT
    lagrange = np.ones((QUANT, 8))
    for node_a in range(8):
        for node_b in range(8):
            if node_b != node_a:
                lagrange[:, node_a] *= (points - GLL_NODES[node_b]) / (
                    GLL_NODES[node_a] - GLL_NODES[node_b]
                )
    rest = lagrange.astype(np.float32).T
    pieces = []
    for _ in range(3):
        piece = rest.astype(bf16)
        pieces.append(piece)
        rest = rest - piece.astype(np.float32)
    pieces.append(np.zeros_like(pieces[0]))
    return np.concatenate(pieces, axis=0)


def depth_pieces():
    centres = ((np.arange(BINS_THIRD_AXIS) + 0.5) / BX - 0.5 * HEIGHT) * DEPTH_SCALE
    rows = np.zeros((8, BINS_THIRD_AXIS))
    rows[2] = 2.0 * centres * (DEPTH_SCALE / PAIR_SCALE)
    rows[4] = -centres * centres
    pieces = []
    for _ in range(3):
        piece = rows.astype(bf16)
        pieces.append(piece)
        rows = rows - piece.astype(np.float64)
    first, second, third = pieces
    last = np.zeros((16, BINS_THIRD_AXIS))
    last[0:3] = 1.0
    return np.concatenate([first, first, second, second, first, third, last.astype(bf16)], axis=0)


def rows_iota(shape):
    return lax.broadcasted_iota(jnp.int32, shape, 0)


def split3(x):
    high = x.astype(bf16).astype(f32)
    rest = x - high
    middle = rest.astype(bf16).astype(f32)
    low = (rest - middle).astype(bf16).astype(f32)
    return high, middle, low


def kernel(
    grid_x, grid_y,
    frac_in, vel_in, drag_in, vol_in, owner_in, element_in, coords_in, table_in, basis_in, depth_in,
    force_out, field_out,
    force_ref, field_ref,
    frac_ref, vel_ref, drag_ref, vol_ref, owner_ref, element_ref, coords_ref, table_ref, basis_ref, depth_ref,
    pos_send, pos_recv, req_send, req_recv, val_send, val_recv, load_send, load_recv,
    xs, scaled, close, fq_t, feat, fp, g_ref, weights, own_val, pair_acc, wz, spread_c, spread_e, wx_ref, wy_ref,
    wy4,
    in_ss, out_ss, pos_ss, pos_rs, req_ss, req_rs, val_ss, val_rs, load_ss, load_rs,
):
    inputs = (
        (frac_in, frac_ref), (owner_in, owner_ref), (element_in, element_ref), (coords_in, coords_ref),
        (basis_in, basis_ref), (table_in, table_ref), (vel_in, vel_ref), (drag_in, drag_ref), (vol_in, vol_ref),
        (depth_in, depth_ref),
    )
    loads_in = [pltpu.make_async_copy(src, dst, in_ss.at[k]) for k, (src, dst) in enumerate(inputs)]
    for copy in loads_in:
        copy.start()

    me_x = lax.axis_index("gx")
    me_y = lax.axis_index("gy")
    ids = []
    present = []
    inside = []
    for dx, dy in STEPS:
        tx, ty = me_x + dx, me_y + dy
        ids.append((lax.rem(tx + grid_x, grid_x), lax.rem(ty + grid_y, grid_y)))
        within = (tx >= 0) & (tx < grid_x) & (ty >= 0) & (ty < grid_y)
        inside.append(within)
        present.append(jnp.where(within, 1.0, 0.0).astype(f32))
    groups = ((None, (3, 4)), (me_x > 0, (0, 1, 2)), (me_x < grid_x - 1, (5, 6, 7)))

    def guarded(condition, act):
        if condition is None:
            act()
        else:
            pl.when(condition)(act)

    barrier = pltpu.get_barrier_semaphore()
    neighbours = jnp.int32(0)
    for n in range(8):
        neighbours = neighbours + inside[n].astype(jnp.int32)

        @pl.when(inside[n])
        def _(n=n):
            pl.semaphore_signal(barrier, inc=1, device_id=ids[n], device_id_type=MESH)

        @pl.when(jnp.logical_not(inside[n]))
        def _(n=n):
            pos_recv[n] = jnp.zeros((4, P_DEV), f32)
            load_recv[n] = jnp.zeros((4, P_DEV), f32)
            req_recv[n] = jnp.zeros((8, 128), f32)
            val_recv[n] = jnp.zeros((8, 128), f32)

    def remote(src, dst, ss, rs, n):
        return pltpu.make_async_remote_copy(
            src_ref=src, dst_ref=dst.at[7 - n], send_sem=ss.at[n], recv_sem=rs.at[7 - n],
            device_id=ids[n], device_id_type=MESH,
        )

    pos_copies = [remote(pos_send, pos_recv, pos_ss, pos_rs, n) for n in range(8)]
    req_copies = [remote(req_send.at[n // 2], req_recv, req_ss, req_rs, n) for n in range(8)]
    val_copies = [remote(val_send.at[n // 2], val_recv, val_ss, val_rs, n) for n in range(8)]
    load_copies = [remote(load_send, load_recv, load_ss, load_rs, n) for n in range(8)]

    loads_in[0].wait()
    fz = frac_ref[2]
    z_own = fz * HEIGHT * DEPTH_SCALE

    def sum_step(i, acc):
        at = (rows_iota((64, P_DEV)) + i * 64).astype(f32)
        d = z_own - (at + 0.5) * (DEPTH_SCALE / BX)
        bumps = jnp.exp2(-(d * d))
        return acc + jnp.sum(bumps.reshape(8, 8, P_DEV), axis=0)

    partial = lax.fori_loop(0, BINS_THIRD_AXIS // 64, sum_step, jnp.zeros((8, P_DEV), f32))
    total = jnp.sum(partial, axis=0, keepdims=True)
    for d in range(3):
        pos_send[d : d + 1, :] = frac_ref[d]
    pos_send[3:4, :] = -LOG2E * jnp.log(total)

    def start_all(copies):
        for n in (3, 4, 0, 1, 2, 5, 6, 7):
            pl.when(inside[n])(copies[n].start)

    def arrive(copies, m):
        pl.when(inside[m])(copies[7 - m].wait_recv)

    pl.semaphore_wait(barrier, neighbours)
    start_all(pos_copies)

    for copy in loads_in[1:]:
        copy.wait()
    row8 = rows_iota((8, 1))
    offsets = jnp.zeros((8, 1), jnp.int32)
    for n, (dx, dy) in enumerate(STEPS):
        offsets = jnp.where(row8 == n, dx * grid_y + dy, offsets)
    delta = owner_ref[...] - (me_x * grid_y + me_y)
    chosen = jnp.where(delta == offsets, 1.0, 0.0).astype(f32)
    blocks = [chosen[:, 128 * b : 128 * b + 128] for b in range(8)]
    stacked = jnp.concatenate(blocks, axis=0).astype(bf16)
    lower = rows_iota((128, 128)) < lax.broadcasted_iota(jnp.int32, (128, 128), 1)
    earlier = jnp.dot(stacked, jnp.where(lower, 1.0, 0.0).astype(bf16), preferred_element_type=f32)
    base = (row8 * CAP).astype(f32)
    ranked = []
    for b in range(8):
        ranked.append(earlier[8 * b : 8 * b + 8] + base)
        base = base + jnp.sum(blocks[b], axis=1, keepdims=True)
    ranked = jnp.concatenate(ranked, axis=1)
    is_remote = jnp.sum(chosen, axis=0, keepdims=True)
    place = jnp.sum(chosen * ranked, axis=0, keepdims=True)
    slot = jnp.where(is_remote > 0.0, place, -1.0)
    for i in range(8):
        at = (rows_iota((64, 1)) + i * 64).astype(f32)
        g_ref[64 * i : 64 * i + 64, :] = jnp.where(slot == at, 1.0, 0.0).astype(bf16)

    xs[0:1, :] = element_ref[...].astype(f32)
    for d in range(3):
        xs[1 + d : 2 + d, :] = coords_ref[d].astype(f32)
    xs[4:8, :] = jnp.zeros((4, P_DEV), f32)
    payload = xs[...]
    payload16 = jnp.concatenate([payload, jnp.zeros((8, P_DEV), f32)], axis=0).astype(bf16)
    outgoing = lax.dot_general(
        payload16, g_ref[...], (((1,), (1,)), ((), ())), preferred_element_type=f32
    )
    for j in range(4):
        req_send[j] = outgoing[0:8, 128 * j : 128 * j + 128]

    def interpolate(requests, k):
        slots = requests.shape[1]
        levels = rows_iota((QUANT, 1)).astype(f32)
        factors = []
        for axis in range(3):
            select = jnp.where(requests[1 + axis : 2 + axis, :] == levels, 1.0, 0.0).astype(bf16)
            pieces = jnp.dot(basis_ref[...], select, preferred_element_type=f32)
            factors.append(pieces[0:8] + pieces[8:16] + pieces[16:24])
        for a in range(8):
            plane = factors[0][a : a + 1, :] * factors[1]
            for b in range(0, 8, 2):
                pair = jnp.concatenate(
                    [plane[b : b + 1, :] * factors[2], plane[b + 1 : b + 2, :] * factors[2]], axis=0
                )
                at = 64 * a + 8 * b
                weights[k, at : at + 16, :] = pair.astype(bf16)
        projected = jnp.dot(table_ref[...], weights[k], preferred_element_type=f32)
        mine = requests[0:1, :] == rows_iota((E_DEV, 1)).astype(f32)
        values = [
            jnp.sum(jnp.where(mine, projected[E_DEV * k : E_DEV * k + E_DEV, :], 0.0), axis=0, keepdims=True)
            for k in range(6)
        ]
        values = jnp.concatenate(values + [jnp.zeros((2, slots), f32)], axis=0)
        return values.astype(bf16).astype(f32)

    def place_rows(dx, dy):
        row = rows_iota((8, 1))
        factor = jnp.where(row == 2, HEIGHT * PAIR_SCALE, PAIR_SCALE)
        shift = jnp.where(row == 0, dx * PAIR_SCALE, jnp.where(row == 1, dy * PAIR_SCALE, -0.5 * HEIGHT * PAIR_SCALE))
        return jnp.where(row < 3, xs[...] * factor + shift, 0.0)

    def features(m, dx, dy, weight):
        row = rows_iota((8, 1))
        where_at = place_rows(dx, dy)
        half = 0.5 * jnp.sum(where_at * where_at, axis=0, keepdims=True)
        vector = jnp.where(row == 3, -half, jnp.where(row == 4, 1.0, where_at))
        q1, q2, q3 = split3(vector)
        depth = where_at[2:3, :] * (DEPTH_SCALE / PAIR_SCALE)
        h1, h2, h3 = split3(xs[3:4, :] - depth * depth)
        level = jnp.where(row == 0, h1, jnp.where(row == 1, h2, jnp.where(row == 2, h3, 0.0)))
        stack = jnp.concatenate([q1, q2, q1, q2, q3, q1, level, jnp.zeros_like(level)], axis=0)
        fq_t[m] = stack.T.astype(bf16)
        packed = jnp.where(row < 5, q1, pltpu.roll(q3, 5, axis=0))
        if weight is not None:
            packed, q2 = packed * weight, q2 * weight
        feat[m] = jnp.concatenate([packed, q2], axis=0).astype(bf16)
        return where_at

    xs[0:4, :] = pos_send[...]
    xs[4:8, :] = jnp.zeros((4, P_DEV), f32)
    own_at = features(OWN, 0, 0, None)
    row8 = rows_iota((8, 1))
    half_own = 0.5 * jnp.sum(own_at * own_at, axis=0, keepdims=True)
    p1, p2, p3 = split3(jnp.where(row8 == 3, 1.0, jnp.where(row8 == 4, -half_own, own_at)))
    blank = jnp.zeros_like(p1)
    fp[...] = jnp.concatenate([p1, p1, p2, p2, p1, p3, blank, blank], axis=0).astype(bf16)

    def exponentials(m, turn):
        exponent = jnp.dot(fq_t[m], fp[...], preferred_element_type=f32)
        close[turn] = jnp.exp2(exponent).astype(bf16)

    def pair_sums(m, turn):
        return jnp.dot(feat[m], close[turn], preferred_element_type=f32)

    def edge_rows(fraction, rows):
        d = fraction - (rows.astype(f32) + (0.5 - MARGIN)) * (1.0 / BX)
        return jnp.exp2((d * d) * (-EDGE_RATE))

    row24 = rows_iota((24, 1))
    order_y = jnp.where(row24 < 16, row24 + 4, jnp.where(row24 < 20, row24 - 16, row24))

    def all_edges(m, fx, fy):
        bump_x = edge_rows(fx, row24)
        bump_y = edge_rows(fy, order_y)
        scale_x = 1.0 / jnp.sum(bump_x, axis=0, keepdims=True)
        scale_y = 1.0 / jnp.sum(bump_y, axis=0, keepdims=True)
        wx_ref[m] = bump_x * scale_x
        wy_ref[m] = bump_y * scale_y

    def depth_rows(m):
        exponent = jnp.dot(fq_t[m], depth_ref[...], preferred_element_type=f32)
        wz[m] = jnp.exp2(exponent).astype(bf16)

    exponentials(OWN, 0)
    start_all(req_copies)
    for half in range(2):
        own_val[:, 512 * half : 512 * half + 512] = interpolate(payload[:, 512 * half : 512 * half + 512], half)
    all_edges(OWN, pos_send[0:1, :], pos_send[1:2, :])
    depth_rows(OWN)

    def pair_group(members, turns, before, turn_before, first):
        for m in members:
            arrive(pos_copies, m)
        for m in members:
            xs[0:4, :] = pos_recv[m]
            features(m, STEPS[m][0], STEPS[m][1], present[m])
        acc = None if first else pair_acc[...]
        for m, turn in zip(members, turns):
            term = pair_sums(before, turn_before)
            exponentials(m, turn)
            acc = term if acc is None else acc + term
            before, turn_before = m, turn
        pair_acc[...] = acc

    pair_group((3, 4), (1, 0), OWN, 0, True)

    for m in range(8):
        arrive(req_copies, m)
    low_half = lax.broadcasted_iota(jnp.int32, (8, 128), 1) < CAP
    arrived = jnp.concatenate(
        [jnp.where(low_half, req_recv[2 * j + 1], req_recv[2 * j]) for j in range(4)], axis=1
    )
    served = interpolate(arrived, 2)
    for j in range(4):
        val_send[j] = served[:, 128 * j : 128 * j + 128]
    start_all(val_copies)

    has_lower, has_upper = groups[1][0], groups[2][0]
    guarded(has_lower, lambda: pair_group((0, 1, 2), (1, 0, 1), 4, 0, False))
    block_before = jnp.where(has_lower, 2, 4)
    turn_before = jnp.where(has_lower, 1, 0)
    guarded(has_upper, lambda: pair_group((5, 6, 7), (2, 0, 1), block_before, turn_before, False))
    pair_acc[...] += pair_sums(jnp.where(has_upper, 7, 2), 1)

    for m in range(8):
        arrive(val_copies, m)
    returned = jnp.concatenate(
        [jnp.where(low_half, val_recv[2 * j], val_recv[2 * j + 1]) for j in range(4)], axis=1
    )
    returned16 = jnp.concatenate([returned, jnp.zeros((8, 512), f32)], axis=0).astype(bf16)
    fetched = jnp.dot(returned16, g_ref[...], preferred_element_type=f32)[0:8]
    fetched = jnp.where(is_remote > 0.0, fetched, own_val[...])
    gradient = pltpu.roll(fetched, 5, axis=0)
    sums = pair_acc[...]
    count = sums[4:5, :]
    sums = sums[0:8] + sums[8:16] + pltpu.roll(sums[0:8], 3, axis=0)
    pair = (STIFFNESS / PAIR_SCALE) * (own_at * count - sums)
    for d in range(3):
        xs[d : d + 1, :] = vel_ref[d]
    volume = vol_ref[...]
    force = drag_ref[...] * (fetched - xs[...]) - volume * gradient + pair
    for d in range(3):
        force_ref[d] = force[d : d + 1]
    force_copy = pltpu.make_async_copy(force_ref, force_out, out_ss.at[0])
    force_copy.start()
    loads = jnp.where(row8 == 3, volume, force)
    load_send[...] = loads[0:4]
    start_all(load_copies)

    scaled[...] = load_send[...] * FIELD_SCALE

    def spread_step(a, carry):
        plane = wx_ref[OWN, pl.ds(a + MARGIN, 1), :] * wy_ref[OWN, 0:16, :]
        for c in range(4):
            r0 = pl.multiple_of((c * 16 + a) * 16, 16)
            spread_c[pl.ds(r0, 16), :] = (plane * scaled[c : c + 1, :]).astype(bf16)
        return carry

    lax.fori_loop(0, 16, spread_step, 0)

    for c in range(4):
        part = jnp.dot(spread_c[256 * c : 256 * c + 256, :], wz[OWN], preferred_element_type=f32)
        field_ref[c] = part.reshape(16, 16, BINS_THIRD_AXIS)

    def depth_group(members):
        for m in members:
            all_edges(m, pos_recv[m, 0:1, :], pos_recv[m, 1:2, :])
            depth_rows(m)

    for condition, members in groups:
        guarded(condition, functools.partial(depth_group, members))

    out_copies = [force_copy]

    def write_slabs(first, count, k):
        part = pl.ds(first, count)
        copy = pltpu.make_async_copy(field_ref.at[:, part], field_out.at[:, part], out_ss.at[k])
        copy.start()
        out_copies.append(copy)

    def spread_margin(m, k):
        dx, dy = STEPS[m]
        loads_m = [load_recv[m, c : c + 1, :] * FIELD_SCALE for c in range(4)]
        source_x = {-1: 20, 0: 4, 1: 0}[dx]
        count_x = 16 if dx == 0 else 4
        if dy == 0:
            for a in range(count_x):
                plane = wx_ref[m, source_x + a : source_x + a + 1, :] * wy_ref[m, 0:16, :]
                for c in range(4):
                    r0 = (c * count_x + a) * 16
                    spread_e[k, r0 : r0 + 16, :] = (plane * loads_m[c]).astype(bf16)
        else:
            first = 20 if dy == -1 else 16
            wy4[k, 0:4, :] = wy_ref[m, first : first + 4, :]
            wy4[k, 4:8, :] = wy_ref[m, first : first + 4, :]
            top = rows_iota((8, 1)) < 4
            for a in range(0, count_x, 4):
                planes = []
                for pair_at in (a, a + 2):
                    s = source_x + pair_at
                    planes.append(
                        jnp.where(top, wx_ref[m, s : s + 1, :], wx_ref[m, s + 1 : s + 2, :]) * wy4[k]
                    )
                plane = jnp.concatenate(planes, axis=0)
                for c in range(4):
                    r0 = (c * count_x + a) * 4
                    spread_e[k, r0 : r0 + 16, :] = (plane * loads_m[c]).astype(bf16)

    def product(m, k):
        used = 256 if STEPS[m][1] == 0 or STEPS[m][0] == 0 else 64
        return jnp.dot(spread_e[k, 0:used, :], wz[m], preferred_element_type=f32)

    def add_part(m, part, c):
        dx, dy = STEPS[m]
        target_x = {-1: 0, 0: 0, 1: 12}[dx]
        count_x = 16 if dx == 0 else 4
        if dy == 0:
            field_ref[c, target_x : target_x + 4] += part[64 * c : 64 * c + 64].reshape(4, 16, BINS_THIRD_AXIS)
        else:
            target_y = 0 if dy == -1 else 12
            for a in range(count_x):
                r0 = (c * count_x + a) * 4
                field_ref[c, target_x + a, target_y : target_y + 4, :] += part[r0 : r0 + 4, :]

    def margin_group(members):
        for m in members:
            arrive(load_copies, m)
        for k, m in enumerate(members):
            spread_margin(m, k)
        parts = [product(m, k) for k, m in enumerate(members)]
        for c in range(4):
            for m, part in zip(members, parts):
                add_part(m, part, c)

    for k, (first, count_x) in enumerate(((4, 8), (0, 4), (12, 4))):
        condition, members = groups[k]
        guarded(condition, functools.partial(margin_group, members))
        write_slabs(first, count_x, 1 + k)
    for copy in out_copies:
        copy.wait()
    for copies in (pos_copies, req_copies, val_copies, load_copies):
        for n in range(8):
            pl.when(inside[n])(copies[n].wait_send)


def publish(force_in, field_in, force_out, field_out, force_v, field_v, in_sems, out_sems):
    pairs = [(force_in, force_v, force_out)]
    for c in range(4):
        for k in range(2):
            part = pl.ds(8 * k, 8)
            pairs.append((field_in.at[c, part], field_v.at[c, part], field_out.at[c, part]))
    ins = [pltpu.make_async_copy(a, v, in_sems.at[i]) for i, (a, v, o) in enumerate(pairs)]
    outs = [pltpu.make_async_copy(v, o, out_sems.at[i]) for i, (a, v, o) in enumerate(pairs)]
    for copy in ins:
        copy.start()
    for first, second in zip(ins, outs):
        first.wait()
        second.start()
    for copy in outs:
        copy.wait()


def body(fractions, velocity, drag_rate, volume, owner, element, coords, fluid):
    grid_x = lax.axis_size("gx")
    grid_y = lax.axis_size("gy")
    table = jnp.transpose(fluid.reshape(E_DEV, 6, 512), (1, 0, 2)).reshape(E_DEV * 6, 512)
    hbm = pl.BlockSpec(memory_space=pl.ANY)
    dma = pltpu.SemaphoreType.DMA((8,))
    force, field = pl.pallas_call(
        functools.partial(kernel, grid_x, grid_y),
        out_shape=(
            jax.ShapeDtypeStruct((3, 1, P_DEV), f32),
            jax.ShapeDtypeStruct((4, BX, BY, BINS_THIRD_AXIS), f32),
        ),
        in_specs=[hbm] * 10,
        out_specs=(hbm, hbm),
        scratch_shapes=[
            pltpu.VMEM((3, 1, P_DEV), f32),
            pltpu.VMEM((4, BX, BY, BINS_THIRD_AXIS), f32),
            pltpu.VMEM((3, 1, P_DEV), f32),
            pltpu.VMEM((3, 1, P_DEV), f32),
            pltpu.VMEM((1, P_DEV), f32),
            pltpu.VMEM((1, P_DEV), f32),
            pltpu.VMEM((1, P_DEV), jnp.int32),
            pltpu.VMEM((1, P_DEV), jnp.int32),
            pltpu.VMEM((3, 1, P_DEV), jnp.int32),
            pltpu.VMEM((6 * E_DEV, 512), bf16),
            pltpu.VMEM((32, QUANT), bf16),
            pltpu.VMEM((ROWS_Q, BINS_THIRD_AXIS), bf16),
            pltpu.VMEM((4, P_DEV), f32),
            pltpu.VMEM((8, 4, P_DEV), f32),
            pltpu.VMEM((4, 8, 128), f32),
            pltpu.VMEM((8, 8, 128), f32),
            pltpu.VMEM((4, 8, 128), f32),
            pltpu.VMEM((8, 8, 128), f32),
            pltpu.VMEM((4, P_DEV), f32),
            pltpu.VMEM((8, 4, P_DEV), f32),
            pltpu.VMEM((8, P_DEV), f32),
            pltpu.VMEM((4, P_DEV), f32),
            pltpu.VMEM((3, P_DEV, P_DEV), bf16),
            pltpu.VMEM((9, P_DEV, ROWS_Q), bf16),
            pltpu.VMEM((9, 16, P_DEV), bf16),
            pltpu.VMEM((ROWS_Q, P_DEV), bf16),
            pltpu.VMEM((8 * CAP, P_DEV), bf16),
            pltpu.VMEM((3, 512, 512), bf16),
            pltpu.VMEM((8, P_DEV), f32),
            pltpu.VMEM((16, P_DEV), f32),
            pltpu.VMEM((9, P_DEV, BINS_THIRD_AXIS), bf16),
            pltpu.VMEM((1024, P_DEV), bf16),
            pltpu.VMEM((3, 256, P_DEV), bf16),
            pltpu.VMEM((9, 24, P_DEV), f32),
            pltpu.VMEM((9, 24, P_DEV), f32),
            pltpu.VMEM((3, 8, P_DEV), f32),
        ]
        + [pltpu.SemaphoreType.DMA((10,)), pltpu.SemaphoreType.DMA((4,))] + [dma] * 8,
        compiler_params=pltpu.CompilerParams(
            collective_id=0, has_side_effects=True, vmem_limit_bytes=60 * 1024 * 1024
        ),
        name="particle_step",
    )(
        fractions.reshape(3, 1, P_DEV),
        velocity.reshape(3, 1, P_DEV),
        drag_rate.reshape(1, P_DEV),
        volume.reshape(1, P_DEV),
        owner.reshape(1, P_DEV),
        element.reshape(1, P_DEV),
        coords.reshape(3, 1, P_DEV),
        table,
        jnp.asarray(basis_pieces()),
        jnp.asarray(depth_pieces()),
    )
    force, field = pl.pallas_call(
        publish,
        out_shape=(
            jax.ShapeDtypeStruct((3, 1, P_DEV), f32),
            jax.ShapeDtypeStruct((4, BX, BY, BINS_THIRD_AXIS), f32),
        ),
        in_specs=[hbm] * 2,
        out_specs=(hbm, hbm),
        scratch_shapes=[
            pltpu.VMEM((3, 1, P_DEV), f32),
            pltpu.VMEM((4, BX, BY, BINS_THIRD_AXIS), f32),
            pltpu.SemaphoreType.DMA((17,)),
            pltpu.SemaphoreType.DMA((17,)),
        ],
        compiler_params=pltpu.CompilerParams(vmem_limit_bytes=60 * 1024 * 1024),
        name="publish",
    )(force, field)
    return force.reshape(1, 1, 3, P_DEV), field


def solution(mesh):
    return jax.shard_map(
        body,
        mesh=mesh,
        in_specs=(
            P("gx", "gy", None, None),
            P("gx", "gy", None, None),
            P("gx", "gy", None),
            P("gx", "gy", None),
            P("gx", "gy", None, None),
            P("gx", "gy", None),
            P("gx", "gy", None, None),
            P("gx", "gy", None, None, None),
        ),
        out_specs=(P("gx", "gy", None, None), P(None, "gx", "gy", None)),
        check_vma=False,
    )
```
